256 devices in a mesh: tm: 32 (over z, x_hi, core), grp: 8 (over y, x_lo).
Axes of the slice: x: 4 (x_hi: 2, x_lo: 2; x = x_hi * 2 + x_lo), y: 4, z: 8, core: 2. Of those that a mesh axis runs over, the one named last changes fastest.
Arguments:
- frames_in: bfloat16 [512, 128, 8, 256], P('tm', 'grp'), may hold values from -6 to 6
- span_frames: int32 [32], P('tm'), may hold values from 5 to 13, as said below
- w_spatial: bfloat16 [3, 3, 256, 256], replicated, may hold values from -0.125 to 0.125
- w_temporal: bfloat16 [3, 256, 256], replicated, may hold values from -0.21875 to 0.21875
- w_down: bfloat16 [2, 2, 256, 256], replicated, may hold values from -0.1875 to 0.1875
- cotangent: bfloat16 [512, 64, 4, 256], P('tm', 'grp'), may hold values from -6 to 6
Outputs:
- down_out: bfloat16 [512, 64, 4, 256], P('tm', 'grp')
- grad_x: bfloat16 [512, 128, 8, 256], P('tm', 'grp')
- grad_spatial: float32 [3, 3, 256, 256], replicated
- grad_temporal: float32 [3, 256, 256], replicated
- grad_down: float32 [2, 2, 256, 256], replicated
The draws below stay inside these ranges and needn't reach their ends.
Inputs may be any that keep to these rules, and one draw needn't show every extreme that they name: `span_frames`: each entry is 1 + 4k for a whole k >= 1; some time block uses the largest count 16 - 3.
All inputs are finite; a program needn't handle non-finite values.
Results may differ from the reference program's by a relative error of at most 0.01.
Values may be sent and summed in bfloat16 or wider, within the bound.
A program may use at most 64 MiB of HBM per device.

```python
import jax
import jax.numpy as jnp
from jax import lax

CH = 256
F_CAP = 16
COLS = 8
FRAMES = 512
HEIGHT = 128
N_TM = 32


def draw_span_frames(key, part):
    key = jax.random.fold_in(key, 7)
    steps_key, chosen_key = jax.random.split(key)
    largest = (F_CAP - 4) // 4
    multiples = jax.random.randint(steps_key, (N_TM,), 1, largest + 1)
    chosen = jax.random.randint(chosen_key, (), 0, N_TM)
    multiples = jnp.where(jnp.arange(N_TM) == chosen, largest, multiples)
    return (1 + 4 * multiples).astype(jnp.int32)


def levels(stream_key, shape, cuts, low, high):
    factor_of = 1.0
    for position, shards_of in cuts:
        heights = jax.random.uniform(jax.random.fold_in(jax.random.fold_in(stream_key, 6), position), (shards_of,), jnp.float32, low / len(cuts), high / len(cuts))
        factor_of = factor_of * jnp.repeat(jnp.exp(heights), shape[position] // shards_of).reshape((-1,) + (1,) * (len(shape) - 1 - position))
    return factor_of


def centred(own_key, shape, deviation, limit, shards=(), kind=jnp.bfloat16):
    entries = deviation * jax.random.normal(own_key, shape, jnp.float32)
    if shards:
        entries = entries * levels(own_key, shape, shards, -0.22, 0.18)
    return jnp.clip(entries, -limit, limit).astype(kind)


def setup_inputs(seed: int = 0) -> dict:
    streams_of = jax.random.split(jax.random.key(seed), 7)
    return {
        "frames_in": centred(streams_of[0], (FRAMES, HEIGHT, COLS, CH), 1.0, 6.0, ((0, 32), (1, 8))),
        "span_frames": draw_span_frames(jax.random.fold_in(streams_of[6], 71), 0),
        "w_spatial": centred(streams_of[2], (3, 3, CH, CH), (9 * CH) ** -0.5, 0.125),
        "w_temporal": centred(streams_of[3], (3, CH, CH), (3 * CH) ** -0.5, 0.21875),
        "w_down": centred(streams_of[4], (2, 2, CH, CH), (4 * CH) ** -0.5, 0.1875),
        "cotangent": centred(streams_of[5], (FRAMES, HEIGHT // 2, COLS // 2, CH), 1.0, 6.0, ((0, 32), (1, 8))),
    }


def activate(values):
    scaled = values * lax.rsqrt(lax.optimization_barrier(jnp.mean(values * values, axis=-1, keepdims=True)) + 1e-06)
    return jax.nn.silu(scaled)

def conv_forward(padded, weights, height, width):
    total = None
    for row_off in range(3):
        for col_off in range(3):
            piece = padded[:, row_off:row_off + height, col_off:col_off + width].astype(jnp.float32)
            term = jnp.einsum('fhwc,cd->fhwd', piece, weights[row_off, col_off].astype(jnp.float32))
            total = term if total is None else total + term
    return total

def conv_backward(padded, weights, height, width):
    total = None
    for row_off in range(3):
        for col_off in range(3):
            piece = padded[:, 2 - row_off:2 - row_off + height, 2 - col_off:2 - col_off + width].astype(jnp.float32)
            term = jnp.einsum('fhwd,cd->fhwc', piece, weights[row_off, col_off].astype(jnp.float32))
            total = term if total is None else total + term
    return total

def spatial_grad(padded, grads, height, width):
    rows_out = []
    for row_off in range(3):
        cols_out = []
        for col_off in range(3):
            piece = padded[:, row_off:row_off + height, col_off:col_off + width].astype(jnp.float32)
            cols_out.append(jnp.einsum('fhwc,fhwd->cd', piece, grads.astype(jnp.float32)))
        rows_out.append(jnp.stack(cols_out))
    return jnp.stack(rows_out)

def place(grads, incoming, count):
    anchor = count * 0
    return lax.dynamic_update_slice(grads, incoming, (count, anchor, anchor, anchor))

def reference(frames_in, span_frames, w_spatial, w_temporal, w_down, cotangent):
    frame_ids = jnp.arange(FRAMES, dtype=jnp.int32)
    valid = (frame_ids % F_CAP < span_frames[frame_ids // F_CAP]).astype(jnp.float32)[:, None, None, None]
    x_float = frames_in.astype(jnp.float32)
    activated, pullback = jax.vjp(activate, x_float)
    acts = (activated * valid).astype(jnp.bfloat16)
    acts_pad = jnp.pad(acts, ((0, 0), (1, 1), (1, 1), (0, 0)))
    spatial = conv_forward(acts_pad, w_spatial, HEIGHT, COLS).astype(jnp.bfloat16)
    spat_spans = spatial.reshape(N_TM, F_CAP, HEIGHT, COLS, CH)
    picks = span_frames[:, None] - 2 + jnp.arange(2, dtype=jnp.int32)[None, :]
    edge_frames = jnp.take_along_axis(spat_spans, picks[:, :, None, None, None], axis=1)
    previous = jnp.concatenate([jnp.zeros((1, 2, HEIGHT, COLS, CH), jnp.bfloat16), edge_frames[:-1]], 0)
    extended = jnp.concatenate([previous, spat_spans], 1)
    temporal_sum = None
    for k in range(3):
        term = jnp.einsum('nfhwc,cd->nfhwd', extended[:, k:k + F_CAP].astype(jnp.float32), w_temporal[k].astype(jnp.float32))
        temporal_sum = term if temporal_sum is None else temporal_sum + term
    temporal_sum = temporal_sum.reshape(FRAMES, HEIGHT, COLS, CH)
    y_out = ((x_float + temporal_sum) * valid).astype(jnp.bfloat16)
    y_blocks = y_out.reshape(FRAMES, HEIGHT // 2, 2, COLS // 2, 2, CH).astype(jnp.float32)
    cot_float = cotangent.astype(jnp.float32)
    down_float = w_down.astype(jnp.float32)
    down_out = jnp.einsum('fiajbc,abcd->fijd', y_blocks, down_float).astype(jnp.bfloat16)
    grad_pre = jnp.einsum('fijd,abcd->fiajbc', cot_float, down_float).reshape(FRAMES, HEIGHT, COLS, CH)
    grad_y = (grad_pre * valid).astype(jnp.bfloat16)
    grad_down = jnp.einsum('fiajbc,fijd->abcd', y_blocks, cot_float)
    grad_spans = grad_y.reshape(N_TM, F_CAP, HEIGHT, COLS, CH)
    incoming = jnp.concatenate([grad_spans[1:, :2], jnp.zeros((1, 2, HEIGHT, COLS, CH), jnp.bfloat16)], 0)
    padded_grads = jnp.concatenate([grad_spans, jnp.zeros((N_TM, 2, HEIGHT, COLS, CH), jnp.bfloat16)], 1)
    placed = jax.vmap(place)(padded_grads, incoming, span_frames)
    grad_sum = None
    for k in range(3):
        term = jnp.einsum('nfhwd,cd->nfhwc', placed[:, 2 - k:2 - k + F_CAP].astype(jnp.float32), w_temporal[k].astype(jnp.float32))
        grad_sum = term if grad_sum is None else grad_sum + term
    grad_s = (grad_sum.reshape(FRAMES, HEIGHT, COLS, CH) * valid).astype(jnp.bfloat16)
    grad_temporal = jnp.stack([jnp.einsum('nfhwc,nfhwd->cd', extended[:, k:k + F_CAP].astype(jnp.float32), grad_spans.astype(jnp.float32)) for k in range(3)])
    grads_pad = jnp.pad(grad_s, ((0, 0), (1, 1), (1, 1), (0, 0)))
    grad_a = conv_backward(grads_pad, w_spatial, HEIGHT, COLS)
    grad_spatial = spatial_grad(acts_pad, grad_s, HEIGHT, COLS)
    grad_x = (grad_y.astype(jnp.float32) + valid * pullback(grad_a)[0]).astype(jnp.bfloat16)
    return (down_out, grad_x, grad_spatial, grad_temporal, grad_down)
```

```python
import functools

import jax
import jax.numpy as jnp
from jax import lax
from jax.experimental import pallas as pl
from jax.experimental.pallas import tpu as pltpu
from jax.sharding import PartitionSpec as P

MESH = pl.DeviceIdType.MESH
BF = jnp.bfloat16
F32 = jnp.float32
NT = (((1,), (1,)), ((), ()))
TN = (((0,), (0,)), ((), ()))


def mm(a, b):
    return jnp.dot(a, b, preferred_element_type=F32)


def mm_nt(a, b):
    return lax.dot_general(a, b, NT, preferred_element_type=F32)


def mm_tn(a, b):
    return lax.dot_general(a, b, TN, preferred_element_type=F32)


def onehot(cond):
    return jnp.where(cond, 1.0, 0.0).astype(BF)


def iotas(rows, cols):
    shape = (rows, cols)
    return lax.broadcasted_iota(jnp.int32, shape, 0), lax.broadcasted_iota(jnp.int32, shape, 1)


def kernel(
    n_tm,
    n_grp,
    span,
    x_hbm,
    cot_hbm,
    wsp_hbm,
    wt_hbm,
    wd_hbm,
    down_ref,
    gx_ref,
    gsp_ref,
    gt_ref,
    gd_ref,
    xv,
    cv,
    wsp,
    wt,
    wd,
    perm,
    cown,
    cext,
    gy,
    gyo,
    gs,
    xt,
    acts,
    acts_t,
    edge_rows,
    s_edge,
    s_next,
    r_acts,
    r_cot,
    r_edge,
    r_next,
    sp,
    y4,
    part,
    r_core,
    sum1,
    r_one,
    sum2,
    r_two,
    sum3,
    r_z,
    full,
    in_sem,
    h_send,
    h_recv,
    a_send,
    a_recv,
):
    t = lax.axis_index("tm")
    g = lax.axis_index("grp")
    core = lax.rem(t, 2)
    x = lax.rem(lax.div(t, 2), 2) * 2 + lax.rem(g, 2)
    y = lax.div(g, 2)
    z = lax.div(t, 4)
    count = span[0]

    def device(px, py, pz, pc):
        return (pz * 4 + lax.div(px, 2) * 2 + pc, py * 2 + lax.rem(px, 2))

    def x_peer(d):
        px = lax.rem(x + d, 4)
        return px, device(px, y, z, core)

    def y_peer(d):
        py = lax.rem(y + d, 4)
        return py, device(x, py, z, core)

    def z_peer(d):
        pz = lax.rem(z + d, 8)
        return pz, device(x, y, pz, core)

    sibling = device(x, y, z, 1 - core)
    t_next, t_prev = lax.rem(t + 1, n_tm), lax.rem(t + n_tm - 1, n_tm)
    g_next, g_prev = lax.rem(g + 1, n_grp), lax.rem(g + n_grp - 1, n_grp)

    loads = [
        pltpu.make_async_copy(src, dst, in_sem.at[i])
        for i, (src, dst) in enumerate(
            ((cot_hbm, cv), (x_hbm, xv), (wd_hbm, wd), (wt_hbm, wt), (wsp_hbm, wsp))
        )
    ]
    for load in loads:
        load.start()

    partners = [(t, g_next), (t, g_prev), (t_next, g), (t_prev, g)]
    partners += [(t_next, g_next), (t_next, g_prev), (t_prev, g_next), (t_prev, g_prev)]
    partners += [sibling]
    partners += [x_peer(d)[1] for d in (1, 2, 3)]
    partners += [y_peer(d)[1] for d in (1, 2, 3)]
    partners += [z_peer(d)[1] for d in range(1, 8)]
    barrier = pltpu.get_barrier_semaphore()
    for partner in partners:
        pl.semaphore_signal(barrier, inc=1, device_id=partner, device_id_type=MESH)

    r, q = iotas(256, 256)
    perm[...] = onehot((lax.rem(r, 16) == lax.div(q, 16)) & (lax.div(r, 16) == lax.rem(q, 16)))
    slot = lax.rem(lax.broadcasted_iota(jnp.int32, (256, 256), 0), 16)
    valid = slot < count

    zeros16 = jnp.zeros((18, 16, 256), BF)
    for buffer in (acts, gs):
        buffer[:, 0:16, :] = zeros16
        buffer[:, 144:160, :] = zeros16

    loads[0].wait()
    r, q = iotas(64, 256)
    pick_next = onehot((lax.div(r, 4) == lax.div(q, 16)) & (lax.rem(r, 4) == lax.rem(q, 16)))
    for b in range(2):
        block = mm(perm[...], cv[:, 16 * b : 16 * b + 16, :].reshape(256, 256))
        block = jnp.where(valid, block, 0.0).astype(BF)
        cown[4 * b : 4 * b + 4] = block.reshape(4, 64, 256)
        s_next[4 * b : 4 * b + 4] = mm(pick_next, block).astype(BF).reshape(4, 16, 256)

    def halo(index, src, dst, to):
        return pltpu.make_async_remote_copy(
            src_ref=src,
            dst_ref=dst,
            send_sem=h_send.at[index],
            recv_sem=h_recv.at[index],
            device_id=to,
            device_id_type=MESH,
        )

    cot_halos = [
        halo(0, cown.at[7], r_cot.at[0], (t, g_next)),
        halo(1, cown.at[0], r_cot.at[1], (t, g_prev)),
        halo(2, s_next, r_next.at[pl.ds(1, 8)], (t_prev, g)),
        halo(3, s_next.at[7], r_next.at[0], (t_prev, g_next)),
        halo(4, s_next.at[0], r_next.at[9], (t_prev, g_prev)),
    ]
    act_halos = [
        halo(5, edge_rows.at[1], r_acts.at[0], (t, g_next)),
        halo(6, edge_rows.at[0], r_acts.at[1], (t, g_prev)),
    ]
    edge_halos = [
        halo(7, s_edge, r_edge.at[pl.ds(1, 16)], (t_next, g)),
        halo(8, s_edge.at[15], r_edge.at[0], (t_next, g_next)),
        halo(9, s_edge.at[0], r_edge.at[17], (t_next, g_prev)),
    ]
    pl.semaphore_wait(barrier, len(partners))
    for copy in cot_halos:
        copy.start()

    loads[1].wait()
    r, q = iotas(32, 256)
    pick_edge = onehot(
        (lax.div(r, 2) == lax.div(q, 16)) & (lax.rem(q, 16) == count - 2 + lax.rem(r, 2))
    )

    def activate(pair):
        rows = pl.ds(pl.multiple_of(16 * pair, 16), 16)
        v = mm(perm[...], xv[:, rows, :].reshape(256, 256))
        xt[pl.ds(2 * pair, 2)] = v.astype(BF).reshape(2, 128, 256)
        u = v * lax.rsqrt(jnp.mean(v * v, axis=-1, keepdims=True) + 1e-06)
        a = jnp.where(valid, u / (1.0 + jnp.exp(-u)), 0.0).astype(BF)
        acts[pl.ds(2 * pair + 1, 2), 16:144, :] = a.reshape(2, 128, 256)
        s_edge[pl.ds(2 * pair, 2)] = mm(pick_edge, a).astype(BF).reshape(2, 16, 256)
        return a

    edge_rows[0] = activate(0)[:128]
    edge_rows[1] = activate(7)[128:]
    for copy in act_halos:
        copy.start()

    @pl.loop(1, 7)
    def _(pair):
        activate(pair)

    for copy in edge_halos:
        copy.start()

    r, q = iotas(256, 256)
    eye = onehot(r == q)
    for pair in range(8):
        a = acts[2 * pair + 1 : 2 * pair + 3, 16:144, :].reshape(256, 256)
        acts_t[:, 256 * pair : 256 * pair + 256] = mm_nt(eye, a).astype(BF)

    for copy in cot_halos:
        copy.wait()
    loads[2].wait()
    r, q = iotas(256, 64)
    put_next = onehot(
        (lax.div(r, 16) == lax.div(q, 4))
        & (lax.rem(r, 16) == count + lax.rem(q, 4))
        & (lax.rem(q, 4) < 2)
        & (t < n_tm - 1)
    )
    for b in range(2):
        block = cown[4 * b : 4 * b + 4].reshape(256, 256).astype(F32)
        block += mm(put_next, r_next[4 * b + 1 : 4 * b + 5].reshape(64, 256))
        cext[4 * b + 1 : 4 * b + 5] = block.astype(BF).reshape(4, 64, 256)
    for side, row, inside in ((0, 0, g > 0), (1, 9, g < n_grp - 1)):
        block = r_cot[side].astype(F32) + mm(put_next[:64, :16], r_next[row])
        cext[row] = jnp.where(inside, block, 0.0).astype(BF)
    for i in range(2):
        for j in range(2):
            piece = mm_nt(cext[...].reshape(640, 256), wd[pl.ds((2 * i + j) * 256, 256), :])
            piece = piece.astype(BF).reshape(10, 4, 16, 256)
            for row in range(10):
                gy[2 * row + i, :, j] = piece[row]

    loads[3].wait()
    r, q = iotas(256, 256)
    same = lax.div(r, 16) == lax.div(q, 16)
    r, q = lax.rem(r, 16), lax.rem(q, 16)
    up1, up2 = onehot(same & (q == r + 1)), onehot(same & (q == r + 2))
    wt_back = jnp.concatenate([wt[512:768], wt[256:512], wt[0:256]], axis=1)

    @pl.loop(0, 9)
    def _(k):
        now = gy[pl.ds(2 * k + 1, 2)].reshape(256, 256)
        ext = jnp.concatenate([now, mm(up1, now).astype(BF), mm(up2, now).astype(BF)], axis=1)
        res = jnp.where(valid, mm_nt(ext, wt_back), 0.0).astype(BF)
        gs[pl.ds(2 * k, 2), 16:144, :] = res.reshape(2, 128, 256)

    @pl.loop(0, 8)
    def _(k):
        now = gy[pl.ds(2 * k + 2, 2)].reshape(256, 256).astype(F32)
        gyo[pl.ds(2 * k, 2)] = jnp.where(valid, now, 0.0).astype(BF).reshape(2, 128, 256)

    def keep(block, value):
        value = value.astype(BF)
        part[block // 8, 0, block % 8] = value[:, :128]
        part[block // 8, 1, block % 8] = value[:, 128:]

    for i in range(3):
        for j in range(3):
            piece = gs[2 - i : 18 - i, 16 * (2 - j) : 16 * (2 - j) + 128, :].reshape(2048, 256)
            keep(3 * i + j, mm(acts_t[...], piece))

    def reduction(n):
        def copy(index, src, dst, to):
            return pltpu.make_async_remote_copy(
                src_ref=src,
                dst_ref=dst,
                send_sem=a_send.at[n, index],
                recv_sem=a_recv.at[n, index],
                device_id=to,
                device_id_type=MESH,
            )

        state = {}

        def begin(copies):
            for c in copies:
                c.start()
            state["now"] = copies

        def finish():
            for c in state["now"]:
                c.wait()

        def s0():
            begin([copy(0, part.at[n, 1 - core], r_core.at[n], sibling)])

        def s1():
            finish()

            @pl.loop(0, 8)
            def _(b):
                total = part[n, core, b].astype(F32) + r_core[n, b].astype(F32)
                sum1[n, b] = total.astype(BF)

            copies = []
            for d in (1, 2, 3):
                px, to = x_peer(d)
                copies.append(copy(d, sum1.at[n, px], r_one.at[n, 0, d - 1], to))
                py, to = y_peer(d)
                copies.append(copy(3 + d, sum1.at[n, 4 + py], r_one.at[n, 1, d - 1], to))
            begin(copies)

        def s2():
            finish()
            for k, own in ((0, x), (1, 4 + y)):
                total = sum1[n, own].astype(F32)
                for d in range(3):
                    total += r_one[n, k, d].astype(F32)
                sum2[n, k] = total.astype(BF).reshape(4, 64, 128)
            copies = []
            for d in (1, 2, 3):
                py, to = y_peer(d)
                copies.append(copy(6 + d, sum2.at[n, 0, py], r_two.at[n, 0, d - 1], to))
                px, to = x_peer(d)
                copies.append(copy(9 + d, sum2.at[n, 1, px], r_two.at[n, 1, d - 1], to))
            begin(copies)

        def s3():
            finish()
            for k, own in ((0, y), (1, x)):
                total = sum2[n, k, own].astype(F32)
                for d in range(3):
                    total += r_two[n, k, d].astype(F32)
                sum3[n, 4 * k : 4 * k + 4] = total.astype(BF).reshape(4, 16, 128)
            copies = []
            for d in range(1, 8):
                pz, to = z_peer(d)
                copies.append(copy(12 + d, sum3.at[n, pz], r_z.at[n, d - 1], to))
            begin(copies)

        k = lax.div(z, 4)
        first, second = x * (1 - k) + y * k, y * (1 - k) + x * k

        def s4():
            finish()
            total = sum3[n, z].astype(F32)
            for d in range(7):
                total += r_z[n, d].astype(F32)
            full[n, core, k, first, second, lax.rem(z, 4)] = total.astype(BF)
            mine = full.at[n, core, k, first, second, lax.rem(z, 4)]
            begin([copy(19 + d, mine, mine, z_peer(d)[1]) for d in range(1, 8)])

        def s5():
            finish()
            one, two = full.at[n, core, 0, x, y], full.at[n, core, 1, y, x]
            copies = []
            for d in (1, 2, 3):
                copies.append(copy(26 + d, one, one, y_peer(d)[1]))
                copies.append(copy(29 + d, two, two, x_peer(d)[1]))
            begin(copies)

        def s6():
            finish()
            one, two = full.at[n, core, 0, x], full.at[n, core, 1, y]
            copies = []
            for d in (1, 2, 3):
                copies.append(copy(32 + d, one, one, x_peer(d)[1]))
                copies.append(copy(35 + d, two, two, y_peer(d)[1]))
            begin(copies)

        def s7():
            finish()
            begin([copy(39, full.at[n, core], full.at[n, core], sibling)])

        return [s0, s1, s2, s3, s4, s5, s6, s7, finish]

    red_a, red_b = reduction(0), reduction(1)
    red_a[0]()

    for copy in act_halos:
        copy.wait()
    for copy in edge_halos:
        copy.wait()
    r, q = iotas(256, 32)
    put_edge = onehot(
        (lax.div(r, 16) == lax.div(q, 2)) & (lax.rem(r, 16) == 14 + lax.rem(q, 2)) & (t > 0)
    )
    for k in range(8):
        block = acts[2 * k + 1 : 2 * k + 3, 16:144, :].reshape(256, 256).astype(F32)
        block += mm(put_edge, r_edge[2 * k + 1 : 2 * k + 3].reshape(32, 256))
        acts[2 * k + 1 : 2 * k + 3, 16:144, :] = block.astype(BF).reshape(2, 128, 256)
    for side, row, inside in ((0, 0, g > 0), (1, 17, g < n_grp - 1)):
        block = r_acts[side].astype(F32) + mm(put_edge[:128, :16], r_edge[row])
        acts[row, 16:144, :] = jnp.where(inside, block, 0.0).astype(BF)
    red_a[1]()

    loads[4].wait()
    r, q = iotas(256, 256)
    same = lax.div(r, 16) == lax.div(q, 16)
    r, q = lax.rem(r, 16), lax.rem(q, 16)
    back1 = onehot(same & (q == lax.rem(r + 15, 16)))
    back2 = onehot(same & (q == lax.rem(r + 14, 16)))

    def taps(buffer, start, flip):
        pieces = []
        for i in range(3):
            for j in range(3):
                a, b = (2 - i, 2 - j) if flip else (i, j)
                piece = buffer[pl.ds(start + a, 4), 16 * b : 16 * b + 128, :]
                pieces.append(piece.reshape(512, 256))
        return jnp.concatenate(pieces, axis=1)

    @pl.loop(0, 4)
    def _(k):
        res = mm(taps(acts, 4 * k, False), wsp[...]).astype(BF)
        rows = pl.ds(pl.multiple_of(512 * k, 512), 512)
        sp[2, rows, :] = res
        for half in range(2):
            rows = pl.ds(pl.multiple_of(512 * k + 256 * half, 256), 256)
            now = res[256 * half : 256 * half + 256]
            sp[1, rows, :] = mm(back1, now).astype(BF)
            sp[0, rows, :] = mm(back2, now).astype(BF)

    red_a[2]()

    slot5 = lax.rem(lax.broadcasted_iota(jnp.int32, (512, 256), 0), 16)
    valid5 = slot5 < count

    @pl.loop(0, 4)
    def _(k):
        rows = pl.ds(pl.multiple_of(512 * k, 512), 512)
        ext = jnp.concatenate([sp[0, rows, :], sp[1, rows, :], sp[2, rows, :]], axis=1)
        total = mm(ext, wt[...]) + xt[pl.ds(4 * k, 4)].reshape(512, 256).astype(F32)
        total = jnp.where(valid5, total, 0.0).astype(BF).reshape(2, 2, 4, 2, 16, 256)
        for i in range(2):
            for j in range(2):
                y4[2 * i + j, pl.ds(2 * k, 2)] = total[:, i, :, j].reshape(2, 64, 256)

    red_a[3]()
    for k in range(3):
        keep(9 + k, mm_tn(sp[k], gyo[...].reshape(2048, 256)))
    for k in range(4):
        keep(12 + k, mm_tn(y4[k].reshape(512, 256), cown[...].reshape(512, 256)))
    red_b[0]()
    red_a[4]()
    ext = jnp.concatenate([y4[k].reshape(512, 256) for k in range(4)], axis=1)
    res = mm(ext, wd[...]).astype(BF)
    for b in range(2):
        block = mm(perm[...], res[256 * b : 256 * b + 256]).astype(BF)
        down_ref[:, 16 * b : 16 * b + 16, :] = block.reshape(16, 16, 256)
    red_b[1]()
    red_a[5]()

    wsp_back = jnp.concatenate([wsp[256 * k : 256 * k + 256] for k in range(9)], axis=1)

    def finish_rows(k):
        ga = mm_nt(taps(gs, 4 * k, True), wsp_back)
        v = xt[pl.ds(4 * k, 4)].reshape(512, 256).astype(F32)
        inv = lax.rsqrt(jnp.mean(v * v, axis=-1, keepdims=True) + 1e-06)
        u = v * inv
        s = 1.0 / (1.0 + jnp.exp(-u))
        gu = ga * (s * (1.0 + u * (1.0 - s)))
        gv = inv * (gu - u * jnp.mean(gu * u, axis=-1, keepdims=True))
        res = gv + gyo[pl.ds(4 * k, 4)].reshape(512, 256).astype(F32)
        res = jnp.where(valid5, res, 0.0).astype(BF)
        for half in range(2):
            block = mm(perm[...], res[256 * half : 256 * half + 256]).astype(BF)
            rows = pl.ds(pl.multiple_of(32 * k + 16 * half, 16), 16)
            gx_ref[:, rows, :] = block.reshape(16, 16, 256)

    pl.loop(0, 2)(finish_rows)
    red_b[2]()
    red_a[6]()
    pl.loop(2, 4)(finish_rows)
    red_b[3]()
    red_a[7]()
    for step in range(4, 9):
        red_b[step]()
    red_a[8]()
    for block in range(16):
        for half in range(2):
            value = full[block // 8, half, block % 8 // 4, block % 4].reshape(256, 128)
            if block < 9:
                gsp_ref[block, :, 128 * half : 128 * half + 128] = value
            elif block < 12:
                gt_ref[block - 9, :, 128 * half : 128 * half + 128] = value
            else:
                gd_ref[block - 12, :, 128 * half : 128 * half + 128] = value


def solution(mesh):
    n_tm, n_grp = mesh.shape["tm"], mesh.shape["grp"]

    def body(frames_in, span_frames, w_spatial, w_temporal, w_down, cotangent):
        hbm = pl.BlockSpec(memory_space=pl.ANY)
        vmem = pl.BlockSpec(memory_space=pltpu.VMEM)
        scratch = [
            pltpu.VMEM((16, 128, 256), BF),
            pltpu.VMEM((16, 32, 256), BF),
            pltpu.VMEM((2304, 256), BF),
            pltpu.VMEM((768, 256), BF),
            pltpu.VMEM((1024, 256), BF),
            pltpu.VMEM((256, 256), BF),
            pltpu.VMEM((8, 64, 256), BF),
            pltpu.VMEM((10, 64, 256), BF),
            pltpu.VMEM((20, 4, 2, 16, 256), BF),
            pltpu.VMEM((16, 128, 256), BF),
            pltpu.VMEM((18, 160, 256), BF),
            pltpu.VMEM((16, 128, 256), BF),
            pltpu.VMEM((18, 160, 256), BF),
            pltpu.VMEM((256, 2048), BF),
            pltpu.VMEM((2, 128, 256), BF),
            pltpu.VMEM((16, 16, 256), BF),
            pltpu.VMEM((8, 16, 256), BF),
            pltpu.VMEM((2, 128, 256), BF),
            pltpu.VMEM((2, 64, 256), BF),
            pltpu.VMEM((18, 16, 256), BF),
            pltpu.VMEM((10, 16, 256), BF),
            pltpu.VMEM((3, 2048, 256), BF),
            pltpu.VMEM((4, 8, 64, 256), BF),
            pltpu.VMEM((2, 2, 8, 256, 128), BF),
            pltpu.VMEM((2, 8, 256, 128), BF),
            pltpu.VMEM((2, 8, 256, 128), BF),
            pltpu.VMEM((2, 2, 3, 256, 128), BF),
            pltpu.VMEM((2, 2, 4, 64, 128), BF),
            pltpu.VMEM((2, 2, 3, 64, 128), BF),
            pltpu.VMEM((2, 8, 16, 128), BF),
            pltpu.VMEM((2, 7, 16, 128), BF),
            pltpu.VMEM((2, 2, 2, 4, 4, 4, 16, 128), BF),
            pltpu.SemaphoreType.DMA((5,)),
            pltpu.SemaphoreType.DMA((10,)),
            pltpu.SemaphoreType.DMA((10,)),
            pltpu.SemaphoreType.DMA((2, 40)),
            pltpu.SemaphoreType.DMA((2, 40)),
        ]
        down, gx, gsp, gt, gd = pl.pallas_call(
            functools.partial(kernel, n_tm, n_grp),
            out_shape=(
                jax.ShapeDtypeStruct((16, 32, 256), BF),
                jax.ShapeDtypeStruct((16, 128, 256), BF),
                jax.ShapeDtypeStruct((9, 256, 256), BF),
                jax.ShapeDtypeStruct((3, 256, 256), BF),
                jax.ShapeDtypeStruct((4, 256, 256), BF),
            ),
            in_specs=[pl.BlockSpec(memory_space=pltpu.SMEM)] + [hbm] * 5,
            out_specs=(vmem,) * 5,
            scratch_shapes=scratch,
            compiler_params=pltpu.CompilerParams(
                collective_id=0, has_side_effects=True, vmem_limit_bytes=52 * 1024 * 1024
            ),
        )(
            span_frames,
            frames_in.reshape(16, 128, 256),
            cotangent.reshape(16, 32, 256),
            w_spatial.reshape(2304, 256),
            w_temporal.reshape(768, 256),
            w_down.reshape(1024, 256),
        )
        return (
            down.reshape(16, 8, 4, 256),
            gx.reshape(16, 16, 8, 256),
            gsp.astype(F32).reshape(3, 3, 256, 256),
            gt.astype(F32),
            gd.astype(F32).reshape(2, 2, 256, 256),
        )

    return jax.shard_map(
        body,
        mesh=mesh,
        in_specs=(P("tm", "grp", None, None), P("tm"), P(), P(), P(), P("tm", "grp", None, None)),
        out_specs=(P("tm", "grp", None, None), P("tm", "grp", None, None), P(), P(), P()),
        check_vma=False,
    )
```

```python
import functools

import jax
import jax.numpy as jnp
from jax import lax
from jax.experimental import pallas as pl
from jax.experimental.pallas import tpu as pltpu
from jax.sharding import PartitionSpec as P

MESH = pl.DeviceIdType.MESH
BF = jnp.bfloat16
F32 = jnp.float32
NT = (((1,), (1,)), ((), ()))
TN = (((0,), (0,)), ((), ()))


def mm(a, b):
    return jnp.dot(a, b, preferred_element_type=F32)


def mm_nt(a, b):
    return lax.dot_general(a, b, NT, preferred_element_type=F32)


def mm_tn(a, b):
    return lax.dot_general(a, b, TN, preferred_element_type=F32)


def onehot(cond):
    return jnp.where(cond, 1.0, 0.0).astype(BF)


def iotas(rows, cols):
    shape = (rows, cols)
    return lax.broadcasted_iota(jnp.int32, shape, 0), lax.broadcasted_iota(jnp.int32, shape, 1)


def kernel(
    n_tm,
    n_grp,
    span,
    x_hbm,
    x_rows,
    cot_hbm,
    wsp_hbm,
    wt_hbm,
    wd_hbm,
    down_v,
    gx_v,
    full,
    xv,
    cv,
    wsp,
    wt,
    wd,
    perm,
    cown,
    cext,
    gy,
    gyo,
    gyo_t,
    cown_t,
    gs,
    xt,
    acts,
    acts_t,
    s_edge,
    s_corner,
    r_x,
    r_edge,
    r_corner,
    r_cot,
    r_next,
    r_ncorner,
    sp,
    y4,
    part,
    r_core,
    sum1,
    r_one,
    sum2,
    r_two,
    in_sem,
    h_send,
    h_recv,
    a_send,
    a_recv,
):
    t = lax.axis_index("tm")
    g = lax.axis_index("grp")
    core = lax.rem(t, 2)
    x = lax.rem(lax.div(t, 2), 2) * 2 + lax.rem(g, 2)
    y = lax.div(g, 2)
    z = lax.div(t, 4)
    count = span[0]

    def device(px, py, pz, pc):
        return (pz * 4 + lax.div(px, 2) * 2 + pc, py * 2 + lax.rem(px, 2))

    line = x * (1 - core) + y * core
    cross = y * (1 - core) + x * core

    def line_peer(d):
        px, py = lax.rem(x + d * (1 - core), 4), lax.rem(y + d * core, 4)
        return lax.rem(line + d, 4), device(px, py, z, core)

    def plane_peer(d, dz):
        px, py = lax.rem(x + d * core, 4), lax.rem(y + d * (1 - core), 4)
        pz = lax.rem(z + dz, 8)
        return lax.rem(cross + d, 4) * 8 + pz, device(px, py, pz, core)

    plane = [(d, dz) for d in (2, 1, 3, 0) for dz in (4, 3, 5, 2, 6, 1, 7, 0) if d + dz]
    mine = cross * 8 + z

    sibling = device(x, y, z, 1 - core)
    t_next, t_prev = lax.rem(t + 1, n_tm), lax.rem(t + n_tm - 1, n_tm)
    g_next, g_prev = lax.rem(g + 1, n_grp), lax.rem(g + n_grp - 1, n_grp)

    loads = [
        pltpu.make_async_copy(src, dst, in_sem.at[i])
        for i, (src, dst) in enumerate(
            ((cot_hbm, cv), (x_hbm, xv), (wd_hbm, wd), (wt_hbm, wt), (wsp_hbm, wsp))
        )
    ]
    for load in loads:
        load.start()

    partners = [(t, g_next), (t, g_prev), (t_next, g), (t_prev, g)]
    partners += [(t_next, g_next), (t_next, g_prev), (t_prev, g_next), (t_prev, g_prev)]
    partners += [sibling]
    partners += [line_peer(d)[1] for d in (1, 2, 3)]
    partners += [plane_peer(d, dz)[1] for d, dz in plane]
    barrier = pltpu.get_barrier_semaphore()
    for partner in partners:
        pl.semaphore_signal(barrier, inc=1, device_id=partner, device_id_type=MESH)

    r, q = iotas(256, 256)
    perm[...] = onehot((lax.rem(r, 16) == lax.div(q, 16)) & (lax.div(r, 16) == lax.rem(q, 16)))
    slot = lax.rem(lax.broadcasted_iota(jnp.int32, (256, 256), 0), 16)
    valid = slot < count

    zeros16 = jnp.zeros((18, 16, 256), BF)
    r_x[:, 13:16] = jnp.zeros((2, 3, 8, 256), BF)
    r_cot[:, 13:16] = jnp.zeros((2, 3, 4, 256), BF)
    for buffer in (acts, gs):
        buffer[:, 0:16, :] = zeros16
        buffer[:, 144:160, :] = zeros16

    def halo(index, src, dst, to):
        return pltpu.make_async_remote_copy(
            src_ref=src,
            dst_ref=dst,
            send_sem=h_send.at[index],
            recv_sem=h_recv.at[index],
            device_id=to,
            device_id_type=MESH,
        )

    used, first = pl.ds(0, 13), cot_hbm.at[pl.ds(0, 2)]
    cot_halos = [
        halo(0, cot_hbm.at[used, 7], r_cot.at[0, used], (t, g_next)),
        halo(1, cot_hbm.at[used, 0], r_cot.at[1, used], (t, g_prev)),
        halo(2, first, r_next, (t_prev, g)),
        halo(3, first.at[:, 7], r_ncorner.at[0], (t_prev, g_next)),
        halo(4, first.at[:, 0], r_ncorner.at[1], (t_prev, g_prev)),
    ]
    act_halos = [
        halo(5, x_rows.at[used, 15], r_x.at[0, used], (t, g_next)),
        halo(6, x_rows.at[used, 0], r_x.at[1, used], (t, g_prev)),
    ]
    edge_halos = [
        halo(7, s_edge, r_edge, (t_next, g)),
        halo(8, s_corner.at[0], r_corner.at[0], (t_next, g_next)),
        halo(9, s_corner.at[1], r_corner.at[1], (t_next, g_prev)),
    ]
    pl.semaphore_wait(barrier, len(partners))
    for copy in cot_halos + act_halos:
        copy.start()
    loads[1].wait()
    last = pl.ds(jnp.clip(count - 2, 0, 14), 2)
    s_edge[...] = xv[last]
    s_corner[0] = xv[last, 120:128, :].reshape(16, 256)
    s_corner[1] = xv[last, 0:8, :].reshape(16, 256)
    for copy in edge_halos:
        copy.start()

    def act(v):
        u = v * lax.rsqrt(jnp.mean(v * v, axis=-1, keepdims=True) + 1e-06)
        return u / (1.0 + jnp.exp(-u))

    r, q = iotas(256, 256)
    eye = onehot(r == q)
    for pair in range(8):
        v = mm(perm[...], xv[:, 16 * pair : 16 * pair + 16, :].reshape(256, 256))
        xt[2 * pair : 2 * pair + 2] = v.astype(BF).reshape(2, 128, 256)
        a = jnp.where(valid, act(v), 0.0).astype(BF)
        acts[2 * pair + 1 : 2 * pair + 3, 16:144, :] = a.reshape(2, 128, 256)
        acts_t[:, 256 * pair : 256 * pair + 256] = mm_nt(eye, a).astype(BF)

    loads[0].wait()
    for b in range(2):
        block = mm(perm[...], cv[:, 4 * b : 4 * b + 4].reshape(256, 256))
        cown[4 * b : 4 * b + 4] = jnp.where(valid, block, 0.0).astype(BF).reshape(4, 64, 256)

    loads[2].wait()
    for i in range(2):
        for j in range(2):
            tap = wd[pl.ds((2 * i + j) * 256, 256), :]
            piece = mm_nt(cown[...].reshape(512, 256), tap).astype(BF).reshape(8, 4, 16, 256)
            for row in range(8):
                gyo[2 * row + i, :, j] = piece[row]
    for k in range(8):
        now = gyo[2 * k : 2 * k + 2].reshape(256, 256)
        gyo_t[:, 256 * k : 256 * k + 256] = mm_nt(eye, now).astype(BF)
    for k in range(2):
        now = cown[4 * k : 4 * k + 4].reshape(256, 256)
        cown_t[:, 256 * k : 256 * k + 256] = mm_nt(eye, now).astype(BF)

    for copy in cot_halos:
        copy.wait()
    r, q = iotas(256, 32)
    put_next = onehot(
        (lax.div(r, 16) == lax.rem(q, 16))
        & (lax.rem(r, 16) == count + lax.div(q, 16))
        & (t < n_tm - 1)
    )
    for b in range(2):
        block = cown[4 * b : 4 * b + 4].reshape(256, 256).astype(F32)
        block += mm(put_next, r_next[:, 4 * b : 4 * b + 4].reshape(32, 256))
        cext[4 * b + 1 : 4 * b + 5] = block.astype(BF).reshape(4, 64, 256)
    r, q = iotas(64, 64)
    turn = onehot((lax.rem(r, 16) == lax.div(q, 4)) & (lax.div(r, 16) == lax.rem(q, 4)))
    r, q = iotas(64, 8)
    put_corner = onehot(
        (lax.div(r, 16) == lax.rem(q, 4))
        & (lax.rem(r, 16) == count + lax.div(q, 4))
        & (t < n_tm - 1)
    )
    for side, row, inside in ((0, 0, g > 0), (1, 9, g < n_grp - 1)):
        block = jnp.where(valid[:64], mm(turn, r_cot[side].reshape(64, 256)), 0.0)
        block += mm(put_corner, r_ncorner[side].reshape(8, 256))
        cext[row] = jnp.where(inside, block, 0.0).astype(BF)
    for i in range(2):
        for j in range(2):
            piece = mm_nt(cext[...].reshape(640, 256), wd[pl.ds((2 * i + j) * 256, 256), :])
            piece = piece.astype(BF).reshape(10, 4, 16, 256)
            for row in range(10):
                gy[2 * row + i, :, j] = piece[row]

    loads[3].wait()
    r, q = iotas(256, 256)
    same = lax.div(r, 16) == lax.div(q, 16)
    r, q = lax.rem(r, 16), lax.rem(q, 16)
    up1, up2 = onehot(same & (q == r + 1)), onehot(same & (q == r + 2))
    wt_back = jnp.concatenate([wt[512:768], wt[256:512], wt[0:256]], axis=1)

    for k in range(9):
        now = gy[2 * k + 1 : 2 * k + 3].reshape(256, 256)
        ext = jnp.concatenate([now, mm(up1, now).astype(BF), mm(up2, now).astype(BF)], axis=1)
        res = jnp.where(valid, mm_nt(ext, wt_back), 0.0).astype(BF)
        gs[2 * k : 2 * k + 2, 16:144, :] = res.reshape(2, 128, 256)

    def keep(block, value):
        value = value.astype(BF)
        n, k, a = block // 8, block % 8 // 4, block % 4
        part[n, k, a, 0:256] = value[:, :128]
        part[n, k, a, 256:512] = value[:, 128:]

    def reduction(n):
        def copy(index, src, dst, to):
            return pltpu.make_async_remote_copy(
                src_ref=src,
                dst_ref=dst,
                send_sem=a_send.at[n, index],
                recv_sem=a_recv.at[n, index],
                device_id=to,
                device_id_type=MESH,
            )

        cores = [copy(a, part.at[n, 1 - core, a], r_core.at[n, a], sibling) for a in range(4)]
        state = {}

        def begin(copies):
            for c in copies:
                c.start()
            state["now"] = copies

        def finish():
            for c in state["now"]:
                c.wait()

        def ahead(a):
            cores[a].wait()
            total = part[n, core, a].astype(F32) + r_core[n, a].astype(F32)
            sum1[n, a] = total.astype(BF)
            d = lax.rem(a + 4 - line, 4)
            px, py = a * (1 - core) + x * core, y * (1 - core) + a * core

            @pl.when(d != 0)
            def _():
                to = device(px, py, z, core)
                copy(3 + d, sum1.at[n, a], r_one.at[n, d - 1], to).start()

        def s2():
            for d in (1, 2, 3):
                copy(3 + d, sum1.at[n, 0], r_one.at[n, d - 1], line_peer(d)[1]).wait()
            total = sum1[n, line].astype(F32)
            for d in range(3):
                total += r_one[n, d].astype(F32)
            sum2[n] = total.astype(BF).reshape(32, 16, 128)
            copies = []
            for i, (d, dz) in enumerate(plane):
                p, to = plane_peer(d, dz)
                copies.append(copy(7 + i, sum2.at[n, p], r_two.at[n, i], to))
            begin(copies)

        def s3():
            finish()
            total = sum2[n, mine].astype(F32)
            for i in range(31):
                total += r_two[n, i].astype(F32)
            full[n, core, line, mine] = total.astype(BF)
            piece = full.at[n, core, line, mine]
            begin([copy(38 + i, piece, piece, plane_peer(d, dz)[1]) for i, (d, dz) in enumerate(plane)])

        def s4():
            finish()
            piece = full.at[n, core, line]
            state["line"] = [copy(68 + d, piece, piece, line_peer(d)[1]) for d in (1, 3, 2)]
            for c in state["line"]:
                c.start()
            begin([copy(72, piece, piece, sibling)])

        def s5():
            for c, d in zip(state["line"], (1, 3, 2)):
                c.wait()
                piece = full.at[n, core, lax.rem(line + 4 - d, 4)]
                state["now"].append(copy(72 + d, piece, piece, sibling))
                state["now"][-1].start()

        return cores, ahead, [s2, s3, s4, s5, finish]

    cores_a, ahead_a, red_a = reduction(0)
    cores_b, ahead_b, red_b = reduction(1)

    def spatial_grad(tap):
        i, j = tap // 3, tap % 3
        piece = gs[2 - i : 18 - i, 16 * (2 - j) : 16 * (2 - j) + 128, :].reshape(2048, 256)
        keep(tap, mm(acts_t[...], piece))

    for a in range(4):
        spatial_grad(a)
        spatial_grad(4 + a)
        cores_a[a].start()
    spatial_grad(8)
    for a in range(4):
        ahead_a(a)

    for copy in act_halos:
        copy.wait()
    for copy in edge_halos:
        copy.wait()
    r, q = iotas(256, 32)
    put_edge = onehot(
        (lax.div(r, 16) == lax.rem(q, 16)) & (lax.rem(r, 16) == 14 + lax.div(q, 16)) & (t > 0)
    )
    edge_act = act(r_edge[...].reshape(256, 256).astype(F32)).astype(BF).reshape(2, 128, 256)
    for k in range(8):
        block = acts[2 * k + 1 : 2 * k + 3, 16:144, :].reshape(256, 256).astype(F32)
        block += mm(put_edge, edge_act[:, 16 * k : 16 * k + 16].reshape(32, 256))
        acts[2 * k + 1 : 2 * k + 3, 16:144, :] = block.astype(BF).reshape(2, 128, 256)
    r, q = iotas(128, 128)
    turn = onehot((lax.rem(r, 16) == lax.div(q, 8)) & (lax.div(r, 16) == lax.rem(q, 8)))
    r, q = iotas(128, 16)
    put_corner = onehot(
        (lax.div(r, 16) == lax.rem(q, 8)) & (lax.rem(r, 16) == 14 + lax.div(q, 8)) & (t > 0)
    )
    for side, row, inside in ((0, 0, g > 0), (1, 17, g < n_grp - 1)):
        block = jnp.where(valid[:128], act(mm(turn, r_x[side].reshape(128, 256))), 0.0)
        block += mm(put_corner, act(r_corner[side].astype(F32)).astype(BF))
        acts[row, 16:144, :] = jnp.where(inside, block, 0.0).astype(BF)

    loads[4].wait()
    r, q = iotas(256, 256)
    same = lax.div(r, 16) == lax.div(q, 16)
    r, q = lax.rem(r, 16), lax.rem(q, 16)
    back1 = onehot(same & (q == lax.rem(r + 15, 16)))
    back2 = onehot(same & (q == lax.rem(r + 14, 16)))

    def taps(buffer, start, flip):
        pieces = []
        for i in range(3):
            for j in range(3):
                a, b = (2 - i, 2 - j) if flip else (i, j)
                piece = buffer[pl.ds(start + a, 4), 16 * b : 16 * b + 128, :]
                pieces.append(piece.reshape(512, 256))
        return jnp.concatenate(pieces, axis=1)

    slot5 = lax.rem(lax.broadcasted_iota(jnp.int32, (512, 256), 0), 16)
    valid5 = slot5 < count
    for k in range(4):
        res = mm(taps(acts, 4 * k, False), wsp[...]).astype(BF)
        one = [mm(back1, res[h : h + 256]).astype(BF) for h in (0, 256)]
        two = [mm(back2, res[h : h + 256]).astype(BF) for h in (0, 256)]
        one, two = jnp.concatenate(one, axis=0), jnp.concatenate(two, axis=0)
        sp[0, 512 * k : 512 * k + 512] = two
        sp[1, 512 * k : 512 * k + 512] = one
        sp[2, 512 * k : 512 * k + 512] = res
        total = mm(jnp.concatenate([two, one, res], axis=1), wt[...])
        total += xt[4 * k : 4 * k + 4].reshape(512, 256).astype(F32)
        total = jnp.where(valid5, total, 0.0).astype(BF).reshape(2, 2, 4, 2, 16, 256)
        for i in range(2):
            for j in range(2):
                y4[2 * i + j, 2 * k : 2 * k + 2] = total[:, i, :, j].reshape(2, 64, 256)

    for k in range(4):
        if k:
            keep(8 + k, mm(gyo_t[...], sp[k - 1]).T)
        keep(12 + k, mm(cown_t[...], y4[k].reshape(512, 256)).T)
        cores_b[k].start()
    for k in range(4):
        ahead_b(k)
    red_a[0]()
    ext = jnp.concatenate([y4[k].reshape(512, 256) for k in range(4)], axis=1)
    res = mm(ext, wd[...]).astype(BF)
    for b in range(2):
        block = mm(perm[...], res[256 * b : 256 * b + 256]).astype(BF)
        down_v[:, 16 * b : 16 * b + 16, :] = block.reshape(16, 16, 256)

    wsp_back = jnp.concatenate([wsp[256 * k : 256 * k + 256] for k in range(9)], axis=1)

    def finish_rows(k):
        ga = mm_nt(taps(gs, 4 * k, True), wsp_back)
        v = xt[pl.ds(4 * k, 4)].reshape(512, 256).astype(F32)
        inv = lax.rsqrt(jnp.mean(v * v, axis=-1, keepdims=True) + 1e-06)
        u = v * inv
        s = 1.0 / (1.0 + jnp.exp(-u))
        gu = ga * (s * (1.0 + u * (1.0 - s)))
        gv = inv * (gu - u * jnp.mean(gu * u, axis=-1, keepdims=True))
        res = gv + gyo[pl.ds(4 * k, 4)].reshape(512, 256).astype(F32)
        res = jnp.where(valid5, res, 0.0).astype(BF)
        for half in range(2):
            block = mm(perm[...], res[256 * half : 256 * half + 256]).astype(BF)
            rows = pl.ds(pl.multiple_of(32 * k + 16 * half, 16), 16)
            gx_v[:, rows, :] = block.reshape(16, 16, 256)

    pl.loop(0, 1)(finish_rows)
    red_b[0]()
    pl.loop(1, 2)(finish_rows)
    red_a[1]()
    pl.loop(2, 3)(finish_rows)
    red_b[1]()
    pl.loop(3, 4)(finish_rows)
    for step in (2, 3, 4):
        red_a[step]()
        red_b[step]()


def results(down, gx, full, down_out, gx_out, gsp_out, gt_out, gd_out, wide, cells, sem):
    copies = [pltpu.make_async_copy(gx, gx_out, sem.at[16])]
    copies[0].start()
    for block in range(16):
        for half in range(2):
            part = full[block // 8, block % 8 // 4, block % 4, 16 * half : 16 * half + 16]
            wide[block, :, 128 * half : 128 * half + 128] = part.reshape(256, 128).astype(F32)
        out = gsp_out.at[block] if block < 9 else gt_out.at[block - 9] if block < 12 else gd_out.at[block - 12]
        copies.append(pltpu.make_async_copy(wide.at[block], out, sem.at[block]))
        copies[-1].start()
    cells[...] = down[...].reshape(16, 8, 4, 256)
    copies.append(pltpu.make_async_copy(cells, down_out, sem.at[17]))
    copies[-1].start()
    for copy in copies:
        copy.wait()


def solution(mesh):
    n_tm, n_grp = mesh.shape["tm"], mesh.shape["grp"]

    def body(frames_in, span_frames, w_spatial, w_temporal, w_down, cotangent):
        hbm = pl.BlockSpec(memory_space=pltpu.HBM)
        vmem = pl.BlockSpec(memory_space=pltpu.VMEM)
        scratch = [
            pltpu.VMEM((16, 128, 256), BF),
            pltpu.VMEM((16, 8, 4, 256), BF),
            pltpu.VMEM((2304, 256), BF),
            pltpu.VMEM((768, 256), BF),
            pltpu.VMEM((1024, 256), BF),
            pltpu.VMEM((256, 256), BF),
            pltpu.VMEM((8, 64, 256), BF),
            pltpu.VMEM((10, 64, 256), BF),
            pltpu.VMEM((20, 4, 2, 16, 256), BF),
            pltpu.VMEM((16, 4, 2, 16, 256), BF),
            pltpu.VMEM((256, 2048), BF),
            pltpu.VMEM((256, 512), BF),
            pltpu.VMEM((18, 160, 256), BF),
            pltpu.VMEM((16, 128, 256), BF),
            pltpu.VMEM((18, 160, 256), BF),
            pltpu.VMEM((256, 2048), BF),
            pltpu.VMEM((2, 128, 256), BF),
            pltpu.VMEM((2, 16, 256), BF),
            pltpu.VMEM((2, 16, 8, 256), BF),
            pltpu.VMEM((2, 128, 256), BF),
            pltpu.VMEM((2, 16, 256), BF),
            pltpu.VMEM((2, 16, 4, 256), BF),
            pltpu.VMEM((2, 8, 4, 256), BF),
            pltpu.VMEM((2, 2, 4, 256), BF),
            pltpu.VMEM((3, 2048, 256), BF),
            pltpu.VMEM((4, 8, 64, 256), BF),
            pltpu.VMEM((2, 2, 4, 512, 128), BF),
            pltpu.VMEM((2, 4, 512, 128), BF),
            pltpu.VMEM((2, 4, 512, 128), BF),
            pltpu.VMEM((2, 3, 512, 128), BF),
            pltpu.VMEM((2, 32, 16, 128), BF),
            pltpu.VMEM((2, 31, 16, 128), BF),
            pltpu.SemaphoreType.DMA((5,)),
            pltpu.SemaphoreType.DMA((10,)),
            pltpu.SemaphoreType.DMA((10,)),
            pltpu.SemaphoreType.DMA((2, 76)),
            pltpu.SemaphoreType.DMA((2, 76)),
        ]
        down, gx, full = pl.pallas_call(
            functools.partial(kernel, n_tm, n_grp),
            out_shape=(
                pltpu.VMEM((16, 32, 256), BF),
                pltpu.VMEM((16, 128, 256), BF),
                pltpu.VMEM((2, 2, 4, 32, 16, 128), BF),
            ),
            in_specs=[pl.BlockSpec(memory_space=pltpu.SMEM)] + [hbm] * 6,
            out_specs=(vmem,) * 3,
            scratch_shapes=scratch,
            compiler_params=pltpu.CompilerParams(
                collective_id=0, has_side_effects=True, vmem_limit_bytes=42 * 1024 * 1024
            ),
        )(
            span_frames,
            *(
                pltpu.with_memory_space_constraint(value, pltpu.HBM)
                for value in (
                    frames_in.reshape(16, 128, 256),
                    frames_in,
                    cotangent,
                    w_spatial.reshape(2304, 256),
                    w_temporal.reshape(768, 256),
                    w_down.reshape(1024, 256),
                )
            ),
        )
        down, gx, gsp, gt, gd = pl.pallas_call(
            results,
            out_shape=(
                jax.ShapeDtypeStruct((16, 8, 4, 256), BF),
                jax.ShapeDtypeStruct((16, 128, 256), BF),
                jax.ShapeDtypeStruct((9, 256, 256), F32),
                jax.ShapeDtypeStruct((3, 256, 256), F32),
                jax.ShapeDtypeStruct((4, 256, 256), F32),
            ),
            in_specs=[vmem] * 3,
            out_specs=(hbm,) * 5,
            scratch_shapes=[
                pltpu.VMEM((16, 256, 256), F32),
                pltpu.VMEM((16, 8, 4, 256), BF),
                pltpu.SemaphoreType.DMA((18,)),
            ],
            compiler_params=pltpu.CompilerParams(vmem_limit_bytes=24 * 1024 * 1024),
        )(down, gx, full)
        return (
            down,
            gx.reshape(16, 16, 8, 256),
            gsp.reshape(3, 3, 256, 256),
            gt,
            gd.reshape(2, 2, 256, 256),
        )

    return jax.shard_map(
        body,
        mesh=mesh,
        in_specs=(P("tm", "grp", None, None), P("tm"), P(), P(), P(), P("tm", "grp", None, None)),
        out_specs=(P("tm", "grp", None, None), P("tm", "grp", None, None), P(), P(), P()),
        check_vma=False,
    )
```

```python
import functools

import jax
import jax.numpy as jnp
from jax import lax
from jax.experimental import pallas as pl
from jax.experimental.pallas import tpu as pltpu
from jax.sharding import PartitionSpec as P

MESH = pl.DeviceIdType.MESH
BF = jnp.bfloat16
F32 = jnp.float32
NT = (((1,), (1,)), ((), ()))
TN = (((0,), (0,)), ((), ()))


def mm(a, b):
    return jnp.dot(a, b, preferred_element_type=F32)


def mm_nt(a, b):
    return lax.dot_general(a, b, NT, preferred_element_type=F32)


def mm_tn(a, b):
    return lax.dot_general(a, b, TN, preferred_element_type=F32)


def onehot(cond):
    return jnp.where(cond, 1.0, 0.0).astype(BF)


def iotas(rows, cols):
    shape = (rows, cols)
    return lax.broadcasted_iota(jnp.int32, shape, 0), lax.broadcasted_iota(jnp.int32, shape, 1)


def kernel(
    n_tm,
    n_grp,
    span,
    x_hbm,
    x_rows,
    cot_hbm,
    wsp_hbm,
    wt_hbm,
    wd_hbm,
    down_v,
    gx_v,
    full,
    xv,
    cv,
    wsp,
    wt,
    wd,
    perm,
    cown,
    cext,
    gy,
    gyo,
    gyo_t,
    cown_t,
    gs,
    xt,
    acts,
    acts_t,
    s_edge,
    s_corner,
    r_x,
    r_edge,
    r_corner,
    r_cot,
    r_next,
    r_ncorner,
    sp,
    y4,
    grad_a,
    grad_v,
    part,
    r_core,
    sum1,
    r_one,
    sum2,
    r_two,
    in_sem,
    h_send,
    h_recv,
    a_send,
    a_recv,
):
    t = lax.axis_index("tm")
    g = lax.axis_index("grp")
    core = lax.rem(t, 2)
    x = lax.rem(lax.div(t, 2), 2) * 2 + lax.rem(g, 2)
    y = lax.div(g, 2)
    z = lax.div(t, 4)
    count = span[0]

    def device(px, py, pz, pc):
        return (pz * 4 + lax.div(px, 2) * 2 + pc, py * 2 + lax.rem(px, 2))

    line = x * (1 - core) + y * core
    cross = y * (1 - core) + x * core

    def line_peer(d):
        px, py = lax.rem(x + d * (1 - core), 4), lax.rem(y + d * core, 4)
        return lax.rem(line + d, 4), device(px, py, z, core)

    def plane_peer(d, dz):
        px, py = lax.rem(x + d * core, 4), lax.rem(y + d * (1 - core), 4)
        pz = lax.rem(z + dz, 8)
        return lax.rem(cross + d, 4) * 8 + pz, device(px, py, pz, core)

    plane = [(d, dz) for d in (2, 1, 3, 0) for dz in (4, 3, 5, 2, 6, 1, 7, 0) if d + dz]
    mine = cross * 8 + z

    sibling = device(x, y, z, 1 - core)
    t_next, t_prev = lax.rem(t + 1, n_tm), lax.rem(t + n_tm - 1, n_tm)
    g_next, g_prev = lax.rem(g + 1, n_grp), lax.rem(g + n_grp - 1, n_grp)

    loads = [
        pltpu.make_async_copy(src, dst, in_sem.at[i])
        for i, (src, dst) in enumerate(
            ((cot_hbm, cv), (x_hbm, xv), (wd_hbm, wd), (wt_hbm, wt), (wsp_hbm, wsp))
        )
    ]
    for load in loads:
        load.start()

    partners = [(t, g_next), (t, g_prev), (t_next, g), (t_prev, g)]
    partners += [(t_next, g_next), (t_next, g_prev), (t_prev, g_next), (t_prev, g_prev)]
    partners += [sibling]
    partners += [line_peer(d)[1] for d in (1, 2, 3)]
    partners += [plane_peer(d, dz)[1] for d, dz in plane]
    barrier = pltpu.get_barrier_semaphore()
    for partner in partners:
        pl.semaphore_signal(barrier, inc=1, device_id=partner, device_id_type=MESH)

    r, q = iotas(256, 256)
    perm[...] = onehot((lax.rem(r, 16) == lax.div(q, 16)) & (lax.div(r, 16) == lax.rem(q, 16)))
    slot = lax.rem(lax.broadcasted_iota(jnp.int32, (256, 256), 0), 16)
    valid = slot < count

    zeros16 = jnp.zeros((18, 16, 256), BF)
    r_x[:, 13:16] = jnp.zeros((2, 3, 8, 256), BF)
    r_cot[:, 13:16] = jnp.zeros((2, 3, 4, 256), BF)
    for buffer in (acts, gs):
        buffer[:, 0:16, :] = zeros16
        buffer[:, 144:160, :] = zeros16

    def halo(index, src, dst, to):
        return pltpu.make_async_remote_copy(
            src_ref=src,
            dst_ref=dst,
            send_sem=h_send.at[index],
            recv_sem=h_recv.at[index],
            device_id=to,
            device_id_type=MESH,
        )

    used, first = pl.ds(0, 13), cot_hbm.at[pl.ds(0, 2)]
    cot_halos = [
        halo(0, cot_hbm.at[used, 7], r_cot.at[0, used], (t, g_next)),
        halo(1, cot_hbm.at[used, 0], r_cot.at[1, used], (t, g_prev)),
        halo(2, first, r_next, (t_prev, g)),
        halo(3, first.at[:, 7], r_ncorner.at[0], (t_prev, g_next)),
        halo(4, first.at[:, 0], r_ncorner.at[1], (t_prev, g_prev)),
    ]
    act_halos = [
        halo(5, x_rows.at[used, 15], r_x.at[0, used], (t, g_next)),
        halo(6, x_rows.at[used, 0], r_x.at[1, used], (t, g_prev)),
    ]
    edge_halos = [
        halo(7, s_edge, r_edge, (t_next, g)),
        halo(8, s_corner.at[0], r_corner.at[0], (t_next, g_next)),
        halo(9, s_corner.at[1], r_corner.at[1], (t_next, g_prev)),
    ]
    pl.semaphore_wait(barrier, len(partners))
    for copy in cot_halos + act_halos:
        copy.start()
    loads[1].wait()
    last = pl.ds(jnp.clip(count - 2, 0, 14), 2)
    s_edge[...] = xv[last]
    s_corner[0] = xv[last, 120:128, :].reshape(16, 256)
    s_corner[1] = xv[last, 0:8, :].reshape(16, 256)
    for copy in edge_halos:
        copy.start()

    def act(v):
        u = v * lax.rsqrt(jnp.mean(v * v, axis=-1, keepdims=True) + 1e-06)
        return u / (1.0 + jnp.exp(-u))

    r, q = iotas(256, 256)
    eye = onehot(r == q)
    for pair in range(8):
        v = mm(perm[...], xv[:, 16 * pair : 16 * pair + 16, :].reshape(256, 256))
        xt[2 * pair : 2 * pair + 2] = v.astype(BF).reshape(2, 128, 256)
        a = jnp.where(valid, act(v), 0.0).astype(BF)
        acts[2 * pair + 1 : 2 * pair + 3, 16:144, :] = a.reshape(2, 128, 256)
        acts_t[:, 256 * pair : 256 * pair + 256] = mm_nt(eye, a).astype(BF)

    loads[0].wait()
    for b in range(2):
        block = mm(perm[...], cv[:, 4 * b : 4 * b + 4].reshape(256, 256))
        cown[4 * b : 4 * b + 4] = jnp.where(valid, block, 0.0).astype(BF).reshape(4, 64, 256)

    loads[2].wait()
    for i in range(2):
        for j in range(2):
            tap = wd[pl.ds((2 * i + j) * 256, 256), :]
            piece = mm_nt(cown[...].reshape(512, 256), tap).astype(BF).reshape(8, 4, 16, 256)
            for row in range(8):
                gyo[2 * row + i, :, j] = piece[row]
    for k in range(8):
        now = gyo[2 * k : 2 * k + 2].reshape(256, 256)
        gyo_t[:, 256 * k : 256 * k + 256] = mm_nt(eye, now).astype(BF)
    for k in range(2):
        now = cown[4 * k : 4 * k + 4].reshape(256, 256)
        cown_t[:, 256 * k : 256 * k + 256] = mm_nt(eye, now).astype(BF)

    for copy in cot_halos:
        copy.wait()
    r, q = iotas(256, 32)
    put_next = onehot(
        (lax.div(r, 16) == lax.rem(q, 16))
        & (lax.rem(r, 16) == count + lax.div(q, 16))
        & (t < n_tm - 1)
    )
    for b in range(2):
        block = cown[4 * b : 4 * b + 4].reshape(256, 256).astype(F32)
        block += mm(put_next, r_next[:, 4 * b : 4 * b + 4].reshape(32, 256))
        cext[4 * b + 1 : 4 * b + 5] = block.astype(BF).reshape(4, 64, 256)
    r, q = iotas(64, 64)
    turn = onehot((lax.rem(r, 16) == lax.div(q, 4)) & (lax.div(r, 16) == lax.rem(q, 4)))
    r, q = iotas(64, 8)
    put_corner = onehot(
        (lax.div(r, 16) == lax.rem(q, 4))
        & (lax.rem(r, 16) == count + lax.div(q, 4))
        & (t < n_tm - 1)
    )
    for side, row, inside in ((0, 0, g > 0), (1, 9, g < n_grp - 1)):
        block = jnp.where(valid[:64], mm(turn, r_cot[side].reshape(64, 256)), 0.0)
        block += mm(put_corner, r_ncorner[side].reshape(8, 256))
        cext[row] = jnp.where(inside, block, 0.0).astype(BF)
    for i in range(2):
        for j in range(2):
            piece = mm_nt(cext[...].reshape(640, 256), wd[pl.ds((2 * i + j) * 256, 256), :])
            piece = piece.astype(BF).reshape(10, 4, 16, 256)
            for row in range(10):
                gy[2 * row + i, :, j] = piece[row]

    loads[3].wait()
    r, q = iotas(256, 256)
    same = lax.div(r, 16) == lax.div(q, 16)
    r, q = lax.rem(r, 16), lax.rem(q, 16)
    up1, up2 = onehot(same & (q == r + 1)), onehot(same & (q == r + 2))
    wt_back = jnp.concatenate([wt[512:768], wt[256:512], wt[0:256]], axis=1)

    for k in range(9):
        now = gy[2 * k + 1 : 2 * k + 3].reshape(256, 256)
        ext = jnp.concatenate([now, mm(up1, now).astype(BF), mm(up2, now).astype(BF)], axis=1)
        res = jnp.where(valid, mm_nt(ext, wt_back), 0.0).astype(BF)
        gs[2 * k : 2 * k + 2, 16:144, :] = res.reshape(2, 128, 256)

    def keep(block, value):
        value = value.astype(BF)
        n, k, a = block // 8, block % 8 // 4, block % 4
        part[n, k, a, 0:16] = value[:, :128].reshape(16, 16, 128)
        part[n, k, a, 16:32] = value[:, 128:].reshape(16, 16, 128)

    def reduction(n):
        def copy(index, src, dst, to):
            return pltpu.make_async_remote_copy(
                src_ref=src,
                dst_ref=dst,
                send_sem=a_send.at[n, index],
                recv_sem=a_recv.at[n, index],
                device_id=to,
                device_id_type=MESH,
            )

        cores = [copy(a, part.at[n, 1 - core, a], r_core.at[n, a], sibling) for a in range(4)]
        state = {}

        def begin(copies):
            for c in copies:
                c.start()
            state["now"] = copies

        def finish():
            for c in state["now"]:
                c.wait()

        def chunk(e):
            return pl.ds(8 * lax.rem(cross + e, 4), 8)

        def line_copy(d, e):
            a, to = line_peer(d)
            index = 4 + 4 * (d - 1) + e
            return copy(index, sum1.at[n, a, chunk(e)], r_one.at[n, d - 1, chunk(e)], to)

        def s1():
            for a in range(4):
                cores[a].wait()
                total = part[n, core, a].astype(F32) + r_core[n, a].astype(F32)
                sum1[n, a] = total.astype(BF)
            for e in (2, 1, 3, 0):
                for d in (2, 1, 3):
                    line_copy(d, e).start()

        def s2():
            copies = []
            for e in (2, 1, 3, 0):
                for d in (2, 1, 3):
                    line_copy(d, e).wait()
                total = sum1[n, line, chunk(e)].astype(F32)
                for d in range(3):
                    total += r_one[n, d, chunk(e)].astype(F32)
                sum2[n, chunk(e)] = total.astype(BF)
                for i, (d, dz) in enumerate(plane):
                    if d == e:
                        p, to = plane_peer(d, dz)
                        copies.append(copy(16 + i, sum2.at[n, p], r_two.at[n, i], to))
                        copies[-1].start()
            state["now"] = copies

        def s3():
            finish()
            total = sum2[n, mine].astype(F32)
            for i in range(31):
                total += r_two[n, i].astype(F32)
            full[n, core, line, mine] = total.astype(BF)
            piece = full.at[n, core, line, mine]
            begin([copy(47 + i, piece, piece, plane_peer(d, dz)[1]) for i, (d, dz) in enumerate(plane)])

        def s4():
            state["line"], copies = {}, []
            for e in (0, 1, 3, 2):
                for c, (d, dz) in zip(state["now"], plane):
                    if d == e:
                        c.wait()
                piece = full.at[n, core, line, chunk(4 - e)]
                for d in (2, 1, 3):
                    c = copy(78 + 4 * (d - 1) + e, piece, piece, line_peer(d)[1])
                    c.start()
                    state["line"][d, e] = c
                copies.append(copy(90 + e, piece, piece, sibling))
                copies[-1].start()
            state["now"] = copies

        def s5():
            for e in (0, 1, 3, 2):
                for d in (1, 3, 2):
                    state["line"][d, e].wait()
                    piece = full.at[n, core, lax.rem(line + 4 - d, 4), chunk(4 - e)]
                    state["now"].append(copy(94 + 4 * (d - 1) + e, piece, piece, sibling))
                    state["now"][-1].start()

        return cores, s1, [s2, s3, s4, s5, finish]

    cores_a, ahead_a, red_a = reduction(0)
    cores_b, ahead_b, red_b = reduction(1)

    def spatial_grad(tap):
        i, j = tap // 3, tap % 3
        piece = gs[2 - i : 18 - i, 16 * (2 - j) : 16 * (2 - j) + 128, :].reshape(2048, 256)
        keep(tap, mm(acts_t[...], piece))

    for a in range(4):
        spatial_grad(a)
        spatial_grad(4 + a)
        cores_a[a].start()
    spatial_grad(8)
    ahead_a()

    for copy in act_halos:
        copy.wait()
    for copy in edge_halos:
        copy.wait()
    r, q = iotas(256, 32)
    put_edge = onehot(
        (lax.div(r, 16) == lax.rem(q, 16)) & (lax.rem(r, 16) == 14 + lax.div(q, 16)) & (t > 0)
    )
    edge_act = act(r_edge[...].reshape(256, 256).astype(F32)).astype(BF).reshape(2, 128, 256)
    for k in range(8):
        block = acts[2 * k + 1 : 2 * k + 3, 16:144, :].reshape(256, 256).astype(F32)
        block += mm(put_edge, edge_act[:, 16 * k : 16 * k + 16].reshape(32, 256))
        acts[2 * k + 1 : 2 * k + 3, 16:144, :] = block.astype(BF).reshape(2, 128, 256)
    r, q = iotas(128, 128)
    turn = onehot((lax.rem(r, 16) == lax.div(q, 8)) & (lax.div(r, 16) == lax.rem(q, 8)))
    r, q = iotas(128, 16)
    put_corner = onehot(
        (lax.div(r, 16) == lax.rem(q, 8)) & (lax.rem(r, 16) == 14 + lax.div(q, 8)) & (t > 0)
    )
    for side, row, inside in ((0, 0, g > 0), (1, 17, g < n_grp - 1)):
        block = jnp.where(valid[:128], act(mm(turn, r_x[side].reshape(128, 256))), 0.0)
        block += mm(put_corner, act(r_corner[side].astype(F32)).astype(BF))
        acts[row, 16:144, :] = jnp.where(inside, block, 0.0).astype(BF)

    loads[4].wait()
    r, q = iotas(256, 256)
    same = lax.div(r, 16) == lax.div(q, 16)
    r, q = lax.rem(r, 16), lax.rem(q, 16)
    back1 = onehot(same & (q == lax.rem(r + 15, 16)))
    back2 = onehot(same & (q == lax.rem(r + 14, 16)))

    def taps(buffer, start, flip):
        pieces = []
        for i in range(3):
            for j in range(3):
                a, b = (2 - i, 2 - j) if flip else (i, j)
                piece = buffer[start + a : start + a + 2, 16 * b : 16 * b + 128, :]
                pieces.append(piece.reshape(256, 256))
        return jnp.concatenate(pieces, axis=1)

    for k in range(8):
        sp[2, 256 * k : 256 * k + 256] = mm(taps(acts, 2 * k, False), wsp[...]).astype(BF)
    for k in range(8):
        rows = slice(256 * k, 256 * k + 256)
        now = sp[2, rows]
        sp[1, rows] = mm(back1, now).astype(BF)
        sp[0, rows] = mm(back2, now).astype(BF)
    for k in range(8):
        rows = slice(256 * k, 256 * k + 256)
        ext = jnp.concatenate([sp[0, rows], sp[1, rows], sp[2, rows]], axis=1)
        total = mm(ext, wt[...]) + xt[2 * k : 2 * k + 2].reshape(256, 256).astype(F32)
        total = jnp.where(valid, total, 0.0).astype(BF).reshape(2, 4, 2, 16, 256)
        for i in range(2):
            for j in range(2):
                y4[2 * i + j, k] = total[i, :, j].reshape(64, 256)

    for k in range(4):
        if k:
            keep(8 + k, mm(gyo_t[...], sp[k - 1]).T)
        keep(12 + k, mm(cown_t[...], y4[k].reshape(512, 256)).T)
        cores_b[k].start()
    ahead_b()
    red_a[0]()
    ext = jnp.concatenate([y4[k].reshape(512, 256) for k in range(4)], axis=1)
    res = mm(ext, wd[...]).astype(BF)
    for b in range(2):
        block = mm(perm[...], res[256 * b : 256 * b + 256]).astype(BF)
        down_v[:, 16 * b : 16 * b + 16, :] = block.reshape(16, 16, 256)

    wsp_back = jnp.concatenate([wsp[256 * k : 256 * k + 256] for k in range(9)], axis=1)

    def grad_acts(k):
        grad_a[256 * k : 256 * k + 256] = mm_nt(taps(gs, 2 * k, True), wsp_back)

    def grad_rows(k):
        ga = grad_a[256 * k : 256 * k + 256]
        v = xt[2 * k : 2 * k + 2].reshape(256, 256).astype(F32)
        inv = lax.rsqrt(jnp.mean(v * v, axis=-1, keepdims=True) + 1e-06)
        u = v * inv
        s = 1.0 / (1.0 + jnp.exp(-u))
        gu = ga * (s * (1.0 + u * (1.0 - s)))
        gv = inv * (gu - u * jnp.mean(gu * u, axis=-1, keepdims=True))
        res = gv + gyo[2 * k : 2 * k + 2].reshape(256, 256).astype(F32)
        grad_v[256 * k : 256 * k + 256] = jnp.where(valid, res, 0.0).astype(BF)

    def turn_rows(k):
        block = mm(perm[...], grad_v[256 * k : 256 * k + 256]).astype(BF)
        gx_v[:, 16 * k : 16 * k + 16, :] = block.reshape(16, 16, 256)

    for k in range(8):
        grad_acts(k)
    red_b[0]()
    for k in range(4):
        grad_rows(k)
    red_a[1]()
    for k in range(4, 8):
        grad_rows(k)
    red_b[1]()
    for k in range(8):
        turn_rows(k)
    for step in (2, 3, 4):
        red_a[step]()
        red_b[step]()


def results(down, gx, full, down_out, gx_out, gsp_out, gt_out, gd_out, wide, cells, sem):
    copies = [pltpu.make_async_copy(gx, gx_out, sem.at[16])]
    copies[0].start()
    for block in range(16):
        for half in range(2):
            part = full[block // 8, block % 8 // 4, block % 4, 16 * half : 16 * half + 16]
            wide[block, :, 128 * half : 128 * half + 128] = part.reshape(256, 128).astype(F32)
        out = gsp_out.at[block] if block < 9 else gt_out.at[block - 9] if block < 12 else gd_out.at[block - 12]
        copies.append(pltpu.make_async_copy(wide.at[block], out, sem.at[block]))
        copies[-1].start()
    cells[...] = down[...].reshape(16, 8, 4, 256)
    copies.append(pltpu.make_async_copy(cells, down_out, sem.at[17]))
    copies[-1].start()
    for copy in copies:
        copy.wait()


def solution(mesh):
    n_tm, n_grp = mesh.shape["tm"], mesh.shape["grp"]

    def body(frames_in, span_frames, w_spatial, w_temporal, w_down, cotangent):
        hbm = pl.BlockSpec(memory_space=pltpu.HBM)
        vmem = pl.BlockSpec(memory_space=pltpu.VMEM)
        scratch = [
            pltpu.VMEM((16, 128, 256), BF),
            pltpu.VMEM((16, 8, 4, 256), BF),
            pltpu.VMEM((2304, 256), BF),
            pltpu.VMEM((768, 256), BF),
            pltpu.VMEM((1024, 256), BF),
            pltpu.VMEM((256, 256), BF),
            pltpu.VMEM((8, 64, 256), BF),
            pltpu.VMEM((10, 64, 256), BF),
            pltpu.VMEM((20, 4, 2, 16, 256), BF),
            pltpu.VMEM((16, 4, 2, 16, 256), BF),
            pltpu.VMEM((256, 2048), BF),
            pltpu.VMEM((256, 512), BF),
            pltpu.VMEM((18, 160, 256), BF),
            pltpu.VMEM((16, 128, 256), BF),
            pltpu.VMEM((18, 160, 256), BF),
            pltpu.VMEM((256, 2048), BF),
            pltpu.VMEM((2, 128, 256), BF),
            pltpu.VMEM((2, 16, 256), BF),
            pltpu.VMEM((2, 16, 8, 256), BF),
            pltpu.VMEM((2, 128, 256), BF),
            pltpu.VMEM((2, 16, 256), BF),
            pltpu.VMEM((2, 16, 4, 256), BF),
            pltpu.VMEM((2, 8, 4, 256), BF),
            pltpu.VMEM((2, 2, 4, 256), BF),
            pltpu.VMEM((3, 2048, 256), BF),
            pltpu.VMEM((4, 8, 64, 256), BF),
            pltpu.VMEM((2048, 256), F32),
            pltpu.VMEM((2048, 256), BF),
            pltpu.VMEM((2, 2, 4, 32, 16, 128), BF),
            pltpu.VMEM((2, 4, 32, 16, 128), BF),
            pltpu.VMEM((2, 4, 32, 16, 128), BF),
            pltpu.VMEM((2, 3, 32, 16, 128), BF),
            pltpu.VMEM((2, 32, 16, 128), BF),
            pltpu.VMEM((2, 31, 16, 128), BF),
            pltpu.SemaphoreType.DMA((5,)),
            pltpu.SemaphoreType.DMA((10,)),
            pltpu.SemaphoreType.DMA((10,)),
            pltpu.SemaphoreType.DMA((2, 106)),
            pltpu.SemaphoreType.DMA((2, 106)),
        ]
        down, gx, full = pl.pallas_call(
            functools.partial(kernel, n_tm, n_grp),
            out_shape=(
                pltpu.VMEM((16, 32, 256), BF),
                pltpu.VMEM((16, 128, 256), BF),
                pltpu.VMEM((2, 2, 4, 32, 16, 128), BF),
            ),
            in_specs=[pl.BlockSpec(memory_space=pltpu.SMEM)] + [hbm] * 6,
            out_specs=(vmem,) * 3,
            scratch_shapes=scratch,
            compiler_params=pltpu.CompilerParams(
                collective_id=0, has_side_effects=True, vmem_limit_bytes=42 * 1024 * 1024
            ),
        )(
            span_frames,
            *(
                pltpu.with_memory_space_constraint(value, pltpu.HBM)
                for value in (
                    frames_in.reshape(16, 128, 256),
                    frames_in,
                    cotangent,
                    w_spatial.reshape(2304, 256),
                    w_temporal.reshape(768, 256),
                    w_down.reshape(1024, 256),
                )
            ),
        )
        down, gx, gsp, gt, gd = pl.pallas_call(
            results,
            out_shape=(
                jax.ShapeDtypeStruct((16, 8, 4, 256), BF),
                jax.ShapeDtypeStruct((16, 128, 256), BF),
                jax.ShapeDtypeStruct((9, 256, 256), F32),
                jax.ShapeDtypeStruct((3, 256, 256), F32),
                jax.ShapeDtypeStruct((4, 256, 256), F32),
            ),
            in_specs=[vmem] * 3,
            out_specs=(hbm,) * 5,
            scratch_shapes=[
                pltpu.VMEM((16, 256, 256), F32),
                pltpu.VMEM((16, 8, 4, 256), BF),
                pltpu.SemaphoreType.DMA((18,)),
            ],
            compiler_params=pltpu.CompilerParams(vmem_limit_bytes=24 * 1024 * 1024),
        )(down, gx, full)
        return (
            down,
            gx.reshape(16, 16, 8, 256),
            gsp.reshape(3, 3, 256, 256),
            gt,
            gd.reshape(2, 2, 256, 256),
        )

    return jax.shard_map(
        body,
        mesh=mesh,
        in_specs=(P("tm", "grp", None, None), P("tm"), P(), P(), P(), P("tm", "grp", None, None)),
        out_specs=(P("tm", "grp", None, None), P("tm", "grp", None, None), P(), P(), P()),
        check_vma=False,
    )
```

```python
import functools

import jax
import jax.numpy as jnp
from jax import lax
from jax.experimental import pallas as pl
from jax.experimental.pallas import tpu as pltpu
from jax.sharding import PartitionSpec as P

MESH = pl.DeviceIdType.MESH
BF = jnp.bfloat16
F32 = jnp.float32
NT = (((1,), (1,)), ((), ()))
TN = (((0,), (0,)), ((), ()))


def mm(a, b):
    return jnp.dot(a, b, preferred_element_type=F32)


def mm_nt(a, b):
    return lax.dot_general(a, b, NT, preferred_element_type=F32)


def mm_tn(a, b):
    return lax.dot_general(a, b, TN, preferred_element_type=F32)


def onehot(cond):
    return jnp.where(cond, 1.0, 0.0).astype(BF)


def iotas(rows, cols):
    shape = (rows, cols)
    return lax.broadcasted_iota(jnp.int32, shape, 0), lax.broadcasted_iota(jnp.int32, shape, 1)


def kernel(
    n_tm,
    n_grp,
    span,
    x_hbm,
    x_rows,
    cot_hbm,
    wsp_hbm,
    wt_hbm,
    wd_hbm,
    down_v,
    gx_v,
    full,
    xv,
    cv,
    wsp,
    wt,
    wd,
    perm,
    cown,
    cext,
    gy,
    gyo,
    gyo_t,
    cown_t,
    gs,
    xt,
    acts,
    acts_t,
    s_edge,
    s_corner,
    r_x,
    r_edge,
    r_corner,
    r_cot,
    r_next,
    r_ncorner,
    sp,
    y4,
    grad_a,
    grad_v,
    part,
    r_core,
    sum1,
    r_one,
    sum2,
    r_two,
    in_sem,
    h_send,
    h_recv,
    a_send,
    a_recv,
):
    t = lax.axis_index("tm")
    g = lax.axis_index("grp")
    core = lax.rem(t, 2)
    x = lax.rem(lax.div(t, 2), 2) * 2 + lax.rem(g, 2)
    y = lax.div(g, 2)
    z = lax.div(t, 4)
    count = span[0]

    def device(px, py, pz, pc):
        return (pz * 4 + lax.div(px, 2) * 2 + pc, py * 2 + lax.rem(px, 2))

    line = x * (1 - core) + y * core
    cross = y * (1 - core) + x * core

    def line_peer(d):
        px, py = lax.rem(x + d * (1 - core), 4), lax.rem(y + d * core, 4)
        return lax.rem(line + d, 4), device(px, py, z, core)

    def plane_peer(d, dz):
        px, py = lax.rem(x + d * core, 4), lax.rem(y + d * (1 - core), 4)
        pz = lax.rem(z + dz, 8)
        return lax.rem(cross + d, 4) * 8 + pz, device(px, py, pz, core)

    plane = [(d, dz) for d in (2, 1, 3, 0) for dz in (4, 3, 5, 2, 6, 1, 7, 0) if d + dz]
    mine = cross * 8 + z

    sibling = device(x, y, z, 1 - core)
    t_next, t_prev = lax.rem(t + 1, n_tm), lax.rem(t + n_tm - 1, n_tm)
    g_next, g_prev = lax.rem(g + 1, n_grp), lax.rem(g + n_grp - 1, n_grp)

    loads = [
        pltpu.make_async_copy(src, dst, in_sem.at[i])
        for i, (src, dst) in enumerate(
            ((cot_hbm, cv), (x_hbm, xv), (wd_hbm, wd), (wt_hbm, wt), (wsp_hbm, wsp))
        )
    ]
    for load in loads:
        load.start()

    partners = [(t, g_next), (t, g_prev), (t_next, g), (t_prev, g)]
    partners += [(t_next, g_next), (t_next, g_prev), (t_prev, g_next), (t_prev, g_prev)]
    partners += [sibling]
    partners += [line_peer(d)[1] for d in (1, 2, 3)]
    partners += [plane_peer(d, dz)[1] for d, dz in plane]
    barrier = pltpu.get_barrier_semaphore()
    for partner in partners:
        pl.semaphore_signal(barrier, inc=1, device_id=partner, device_id_type=MESH)

    r, q = iotas(256, 256)
    perm[...] = onehot((lax.rem(r, 16) == lax.div(q, 16)) & (lax.div(r, 16) == lax.rem(q, 16)))
    slot = lax.rem(lax.broadcasted_iota(jnp.int32, (256, 256), 0), 16)
    valid = slot < count

    zeros16 = jnp.zeros((18, 16, 256), BF)
    r_x[:, 13:16] = jnp.zeros((2, 3, 8, 256), BF)
    r_cot[:, 13:16] = jnp.zeros((2, 3, 4, 256), BF)
    for buffer in (acts, gs):
        buffer[:, 0:16, :] = zeros16
        buffer[:, 144:160, :] = zeros16

    def halo(index, src, dst, to):
        return pltpu.make_async_remote_copy(
            src_ref=src,
            dst_ref=dst,
            send_sem=h_send.at[index],
            recv_sem=h_recv.at[index],
            device_id=to,
            device_id_type=MESH,
        )

    used, first = pl.ds(0, 13), cot_hbm.at[pl.ds(0, 2)]
    cot_halos = [
        halo(0, cot_hbm.at[used, 7], r_cot.at[0, used], (t, g_next)),
        halo(1, cot_hbm.at[used, 0], r_cot.at[1, used], (t, g_prev)),
        halo(2, first, r_next, (t_prev, g)),
        halo(3, first.at[:, 7], r_ncorner.at[0], (t_prev, g_next)),
        halo(4, first.at[:, 0], r_ncorner.at[1], (t_prev, g_prev)),
    ]
    act_halos = [
        halo(5, x_rows.at[used, 15], r_x.at[0, used], (t, g_next)),
        halo(6, x_rows.at[used, 0], r_x.at[1, used], (t, g_prev)),
    ]
    edge_halos = [
        halo(7, s_edge, r_edge, (t_next, g)),
        halo(8, s_corner.at[0], r_corner.at[0], (t_next, g_next)),
        halo(9, s_corner.at[1], r_corner.at[1], (t_next, g_prev)),
    ]
    pl.semaphore_wait(barrier, len(partners))
    for copy in cot_halos:
        copy.start()
    loads[1].wait()
    last = pl.ds(jnp.clip(count - 2, 0, 14), 2)
    s_edge[...] = xv[last]
    s_corner[0] = xv[last, 120:128, :].reshape(16, 256)
    s_corner[1] = xv[last, 0:8, :].reshape(16, 256)
    for copy in edge_halos + act_halos:
        copy.start()

    def act(v):
        u = v * lax.rsqrt(jnp.mean(v * v, axis=-1, keepdims=True) + 1e-06)
        return u / (1.0 + jnp.exp(-u))

    r, q = iotas(256, 256)
    eye = onehot(r == q)
    for pair in range(8):
        v = mm(perm[...], xv[:, 16 * pair : 16 * pair + 16, :].reshape(256, 256))
        xt[2 * pair : 2 * pair + 2] = v.astype(BF).reshape(2, 128, 256)
        a = jnp.where(valid, act(v), 0.0).astype(BF)
        acts[2 * pair + 1 : 2 * pair + 3, 16:144, :] = a.reshape(2, 128, 256)
        acts_t[:, 256 * pair : 256 * pair + 256] = mm_nt(eye, a).astype(BF)

    loads[0].wait()
    for b in range(2):
        block = mm(perm[...], cv[:, 4 * b : 4 * b + 4].reshape(256, 256))
        cown[4 * b : 4 * b + 4] = jnp.where(valid, block, 0.0).astype(BF).reshape(4, 64, 256)

    loads[2].wait()
    for i in range(2):
        for j in range(2):
            tap = wd[pl.ds((2 * i + j) * 256, 256), :]
            piece = mm_nt(cown[...].reshape(512, 256), tap).astype(BF).reshape(8, 4, 16, 256)
            for row in range(8):
                gyo[2 * row + i, :, j] = piece[row]
    for k in range(8):
        now = gyo[2 * k : 2 * k + 2].reshape(256, 256)
        gyo_t[:, 256 * k : 256 * k + 256] = mm_nt(eye, now).astype(BF)
    for k in range(2):
        now = cown[4 * k : 4 * k + 4].reshape(256, 256)
        cown_t[:, 256 * k : 256 * k + 256] = mm_nt(eye, now).astype(BF)

    for copy in cot_halos:
        copy.wait()
    r, q = iotas(256, 32)
    put_next = onehot(
        (lax.div(r, 16) == lax.rem(q, 16))
        & (lax.rem(r, 16) == count + lax.div(q, 16))
        & (t < n_tm - 1)
    )
    for b in range(2):
        block = cown[4 * b : 4 * b + 4].reshape(256, 256).astype(F32)
        block += mm(put_next, r_next[:, 4 * b : 4 * b + 4].reshape(32, 256))
        cext[4 * b + 1 : 4 * b + 5] = block.astype(BF).reshape(4, 64, 256)
    r, q = iotas(64, 64)
    turn = onehot((lax.rem(r, 16) == lax.div(q, 4)) & (lax.div(r, 16) == lax.rem(q, 4)))
    r, q = iotas(64, 8)
    put_corner = onehot(
        (lax.div(r, 16) == lax.rem(q, 4))
        & (lax.rem(r, 16) == count + lax.div(q, 4))
        & (t < n_tm - 1)
    )
    for side, row, inside in ((0, 0, g > 0), (1, 9, g < n_grp - 1)):
        block = jnp.where(valid[:64], mm(turn, r_cot[side].reshape(64, 256)), 0.0)
        block += mm(put_corner, r_ncorner[side].reshape(8, 256))
        cext[row] = jnp.where(inside, block, 0.0).astype(BF)
    for i in range(2):
        for j in range(2):
            piece = mm_nt(cext[...].reshape(640, 256), wd[pl.ds((2 * i + j) * 256, 256), :])
            piece = piece.astype(BF).reshape(10, 4, 16, 256)
            for row in range(10):
                gy[2 * row + i, :, j] = piece[row]

    loads[3].wait()
    r, q = iotas(256, 256)
    same = lax.div(r, 16) == lax.div(q, 16)
    r, q = lax.rem(r, 16), lax.rem(q, 16)
    up1, up2 = onehot(same & (q == r + 1)), onehot(same & (q == r + 2))
    wt_back = jnp.concatenate([wt[512:768], wt[256:512], wt[0:256]], axis=1)

    for k in range(9):
        now = gy[2 * k + 1 : 2 * k + 3].reshape(256, 256)
        ext = jnp.concatenate([now, mm(up1, now).astype(BF), mm(up2, now).astype(BF)], axis=1)
        res = jnp.where(valid, mm_nt(ext, wt_back), 0.0).astype(BF)
        gs[2 * k : 2 * k + 2, 16:144, :] = res.reshape(2, 128, 256)

    def keep(block, value):
        value = value.astype(BF)
        n, k, a = block // 8, block % 8 // 4, block % 4
        part[n, k, a, 0:16] = value[:, :128].reshape(16, 16, 128)
        part[n, k, a, 16:32] = value[:, 128:].reshape(16, 16, 128)

    def reduction(n):
        def copy(index, src, dst, to):
            return pltpu.make_async_remote_copy(
                src_ref=src,
                dst_ref=dst,
                send_sem=a_send.at[n, index],
                recv_sem=a_recv.at[n, index],
                device_id=to,
                device_id_type=MESH,
            )

        cores = [copy(a, part.at[n, 1 - core, a], r_core.at[n, a], sibling) for a in range(4)]
        state = {}

        def begin(copies):
            for c in copies:
                c.start()
            state["now"] = copies

        def finish():
            for c in state["now"]:
                c.wait()

        def chunk(e):
            return pl.ds(8 * lax.rem(cross + e, 4), 8)

        def line_copy(d, e):
            a, to = line_peer(d)
            index = 4 + 4 * (d - 1) + e
            return copy(index, sum1.at[n, a, chunk(e)], r_one.at[n, d - 1, chunk(e)], to)

        def s1():
            for a in range(4):
                cores[a].wait()
                total = part[n, core, a].astype(F32) + r_core[n, a].astype(F32)
                sum1[n, a] = total.astype(BF)
            for e in (2, 1, 3, 0):
                for d in (2, 1, 3):
                    line_copy(d, e).start()

        def s2():
            copies = []
            for e in (2, 1, 3, 0):
                for d in (2, 1, 3):
                    line_copy(d, e).wait()
                total = sum1[n, line, chunk(e)].astype(F32)
                for d in range(3):
                    total += r_one[n, d, chunk(e)].astype(F32)
                sum2[n, chunk(e)] = total.astype(BF)
                for i, (d, dz) in enumerate(plane):
                    if d == e:
                        p, to = plane_peer(d, dz)
                        copies.append(copy(16 + i, sum2.at[n, p], r_two.at[n, i], to))
                        copies[-1].start()
            state["now"] = copies

        def s3():
            finish()
            total = sum2[n, mine].astype(F32)
            for i in range(31):
                total += r_two[n, i].astype(F32)
            full[n, core, line, mine] = total.astype(BF)
            piece = full.at[n, core, line, mine]
            begin([copy(47 + i, piece, piece, plane_peer(d, dz)[1]) for i, (d, dz) in enumerate(plane)])

        def s4():
            state["line"], copies = {}, []
            for e in (0, 1, 3, 2):
                for c, (d, dz) in zip(state["now"], plane):
                    if d == e:
                        c.wait()
                piece = full.at[n, core, line, chunk(4 - e)]
                for d in (2, 1, 3):
                    c = copy(78 + 4 * (d - 1) + e, piece, piece, line_peer(d)[1])
                    c.start()
                    state["line"][d, e] = c
                copies.append(copy(90 + e, piece, piece, sibling))
                copies[-1].start()
            state["now"] = copies

        def s5():
            for e in (0, 1, 3, 2):
                for d in (1, 3, 2):
                    state["line"][d, e].wait()
                    piece = full.at[n, core, lax.rem(line + 4 - d, 4), chunk(4 - e)]
                    state["now"].append(copy(94 + 4 * (d - 1) + e, piece, piece, sibling))
                    state["now"][-1].start()

        return cores, s1, [s2, s3, s4, s5, finish]

    cores_a, ahead_a, red_a = reduction(0)
    cores_b, ahead_b, red_b = reduction(1)

    def spatial_grad(tap):
        i, j = tap // 3, tap % 3
        piece = gs[2 - i : 18 - i, 16 * (2 - j) : 16 * (2 - j) + 128, :].reshape(2048, 256)
        keep(tap, mm(acts_t[...], piece))

    for a in range(4):
        spatial_grad(a)
        spatial_grad(4 + a)
        cores_a[a].start()
    spatial_grad(8)
    ahead_a()

    for copy in act_halos:
        copy.wait()
    for copy in edge_halos:
        copy.wait()
    r, q = iotas(256, 32)
    put_edge = onehot(
        (lax.div(r, 16) == lax.rem(q, 16)) & (lax.rem(r, 16) == 14 + lax.div(q, 16)) & (t > 0)
    )
    edge_act = act(r_edge[...].reshape(256, 256).astype(F32)).astype(BF).reshape(2, 128, 256)
    for k in range(8):
        block = acts[2 * k + 1 : 2 * k + 3, 16:144, :].reshape(256, 256).astype(F32)
        block += mm(put_edge, edge_act[:, 16 * k : 16 * k + 16].reshape(32, 256))
        acts[2 * k + 1 : 2 * k + 3, 16:144, :] = block.astype(BF).reshape(2, 128, 256)
    r, q = iotas(128, 128)
    turn = onehot((lax.rem(r, 16) == lax.div(q, 8)) & (lax.div(r, 16) == lax.rem(q, 8)))
    r, q = iotas(128, 16)
    put_corner = onehot(
        (lax.div(r, 16) == lax.rem(q, 8)) & (lax.rem(r, 16) == 14 + lax.div(q, 8)) & (t > 0)
    )
    for side, row, inside in ((0, 0, g > 0), (1, 17, g < n_grp - 1)):
        block = jnp.where(valid[:128], act(mm(turn, r_x[side].reshape(128, 256))), 0.0)
        block += mm(put_corner, act(r_corner[side].astype(F32)).astype(BF))
        acts[row, 16:144, :] = jnp.where(inside, block, 0.0).astype(BF)

    loads[4].wait()
    r, q = iotas(256, 256)
    same = lax.div(r, 16) == lax.div(q, 16)
    r, q = lax.rem(r, 16), lax.rem(q, 16)
    back1 = onehot(same & (q == lax.rem(r + 15, 16)))
    back2 = onehot(same & (q == lax.rem(r + 14, 16)))

    def taps(buffer, start, flip):
        pieces = []
        for i in range(3):
            for j in range(3):
                a, b = (2 - i, 2 - j) if flip else (i, j)
                piece = buffer[start + a : start + a + 2, 16 * b : 16 * b + 128, :]
                pieces.append(piece.reshape(256, 256))
        return jnp.concatenate(pieces, axis=1)

    for k in range(8):
        sp[2, 256 * k : 256 * k + 256] = mm(taps(acts, 2 * k, False), wsp[...]).astype(BF)
    for k in range(8):
        rows = slice(256 * k, 256 * k + 256)
        now = sp[2, rows]
        sp[1, rows] = mm(back1, now).astype(BF)
        sp[0, rows] = mm(back2, now).astype(BF)
    for k in range(8):
        rows = slice(256 * k, 256 * k + 256)
        ext = jnp.concatenate([sp[0, rows], sp[1, rows], sp[2, rows]], axis=1)
        total = mm(ext, wt[...]) + xt[2 * k : 2 * k + 2].reshape(256, 256).astype(F32)
        total = jnp.where(valid, total, 0.0).astype(BF).reshape(2, 4, 2, 16, 256)
        for i in range(2):
            for j in range(2):
                y4[2 * i + j, k] = total[i, :, j].reshape(64, 256)

    for k in range(4):
        if k:
            keep(8 + k, mm(gyo_t[...], sp[k - 1]).T)
        keep(12 + k, mm(cown_t[...], y4[k].reshape(512, 256)).T)
        cores_b[k].start()
    ahead_b()
    red_a[0]()
    ext = jnp.concatenate([y4[k].reshape(512, 256) for k in range(4)], axis=1)
    res = mm(ext, wd[...]).astype(BF)
    for b in range(2):
        block = mm(perm[...], res[256 * b : 256 * b + 256]).astype(BF)
        down_v[:, 16 * b : 16 * b + 16, :] = block.reshape(16, 16, 256)

    wsp_back = jnp.concatenate([wsp[256 * k : 256 * k + 256] for k in range(9)], axis=1)

    def grad_acts(k):
        grad_a[256 * k : 256 * k + 256] = mm_nt(taps(gs, 2 * k, True), wsp_back)

    def grad_rows(k):
        ga = grad_a[256 * k : 256 * k + 256]
        v = xt[2 * k : 2 * k + 2].reshape(256, 256).astype(F32)
        inv = lax.rsqrt(jnp.mean(v * v, axis=-1, keepdims=True) + 1e-06)
        u = v * inv
        s = 1.0 / (1.0 + jnp.exp(-u))
        gu = ga * (s * (1.0 + u * (1.0 - s)))
        gv = inv * (gu - u * jnp.mean(gu * u, axis=-1, keepdims=True))
        res = gv + gyo[2 * k : 2 * k + 2].reshape(256, 256).astype(F32)
        grad_v[256 * k : 256 * k + 256] = jnp.where(valid, res, 0.0).astype(BF)

    def turn_rows(k):
        block = mm(perm[...], grad_v[256 * k : 256 * k + 256]).astype(BF)
        gx_v[:, 16 * k : 16 * k + 16, :] = block.reshape(16, 16, 256)

    for k in range(8):
        grad_acts(k)
    red_b[0]()
    for k in range(4):
        grad_rows(k)
    red_a[1]()
    for k in range(4, 8):
        grad_rows(k)
    red_b[1]()
    for k in range(8):
        turn_rows(k)
    for step in (2, 3, 4):
        red_a[step]()
        red_b[step]()


def results(down, gx, full, down_out, gx_out, gsp_out, gt_out, gd_out, wide, cells, sem):
    copies = [pltpu.make_async_copy(gx, gx_out, sem.at[16])]
    copies[0].start()
    for block in range(16):
        for half in range(2):
            part = full[block // 8, block % 8 // 4, block % 4, 16 * half : 16 * half + 16]
            wide[block, :, 128 * half : 128 * half + 128] = part.reshape(256, 128).astype(F32)
        out = gsp_out.at[block] if block < 9 else gt_out.at[block - 9] if block < 12 else gd_out.at[block - 12]
        copies.append(pltpu.make_async_copy(wide.at[block], out, sem.at[block]))
        copies[-1].start()
    cells[...] = down[...].reshape(16, 8, 4, 256)
    copies.append(pltpu.make_async_copy(cells, down_out, sem.at[17]))
    copies[-1].start()
    for copy in copies:
        copy.wait()


def solution(mesh):
    n_tm, n_grp = mesh.shape["tm"], mesh.shape["grp"]

    def body(frames_in, span_frames, w_spatial, w_temporal, w_down, cotangent):
        hbm = pl.BlockSpec(memory_space=pltpu.HBM)
        vmem = pl.BlockSpec(memory_space=pltpu.VMEM)
        scratch = [
            pltpu.VMEM((16, 128, 256), BF),
            pltpu.VMEM((16, 8, 4, 256), BF),
            pltpu.VMEM((2304, 256), BF),
            pltpu.VMEM((768, 256), BF),
            pltpu.VMEM((1024, 256), BF),
            pltpu.VMEM((256, 256), BF),
            pltpu.VMEM((8, 64, 256), BF),
            pltpu.VMEM((10, 64, 256), BF),
            pltpu.VMEM((20, 4, 2, 16, 256), BF),
            pltpu.VMEM((16, 4, 2, 16, 256), BF),
            pltpu.VMEM((256, 2048), BF),
            pltpu.VMEM((256, 512), BF),
            pltpu.VMEM((18, 160, 256), BF),
            pltpu.VMEM((16, 128, 256), BF),
            pltpu.VMEM((18, 160, 256), BF),
            pltpu.VMEM((256, 2048), BF),
            pltpu.VMEM((2, 128, 256), BF),
            pltpu.VMEM((2, 16, 256), BF),
            pltpu.VMEM((2, 16, 8, 256), BF),
            pltpu.VMEM((2, 128, 256), BF),
            pltpu.VMEM((2, 16, 256), BF),
            pltpu.VMEM((2, 16, 4, 256), BF),
            pltpu.VMEM((2, 8, 4, 256), BF),
            pltpu.VMEM((2, 2, 4, 256), BF),
            pltpu.VMEM((3, 2048, 256), BF),
            pltpu.VMEM((4, 8, 64, 256), BF),
            pltpu.VMEM((2048, 256), F32),
            pltpu.VMEM((2048, 256), BF),
            pltpu.VMEM((2, 2, 4, 32, 16, 128), BF),
            pltpu.VMEM((2, 4, 32, 16, 128), BF),
            pltpu.VMEM((2, 4, 32, 16, 128), BF),
            pltpu.VMEM((2, 3, 32, 16, 128), BF),
            pltpu.VMEM((2, 32, 16, 128), BF),
            pltpu.VMEM((2, 31, 16, 128), BF),
            pltpu.SemaphoreType.DMA((5,)),
            pltpu.SemaphoreType.DMA((10,)),
            pltpu.SemaphoreType.DMA((10,)),
            pltpu.SemaphoreType.DMA((2, 106)),
            pltpu.SemaphoreType.DMA((2, 106)),
        ]
        down, gx, full = pl.pallas_call(
            functools.partial(kernel, n_tm, n_grp),
            out_shape=(
                pltpu.VMEM((16, 32, 256), BF),
                pltpu.VMEM((16, 128, 256), BF),
                pltpu.VMEM((2, 2, 4, 32, 16, 128), BF),
            ),
            in_specs=[pl.BlockSpec(memory_space=pltpu.SMEM)] + [hbm] * 6,
            out_specs=(vmem,) * 3,
            scratch_shapes=scratch,
            compiler_params=pltpu.CompilerParams(
                collective_id=0, has_side_effects=True, vmem_limit_bytes=42 * 1024 * 1024
            ),
        )(
            span_frames,
            *(
                pltpu.with_memory_space_constraint(value, pltpu.HBM)
                for value in (
                    frames_in.reshape(16, 128, 256),
                    frames_in,
                    cotangent,
                    w_spatial.reshape(2304, 256),
                    w_temporal.reshape(768, 256),
                    w_down.reshape(1024, 256),
                )
            ),
        )
        down, gx, gsp, gt, gd = pl.pallas_call(
            results,
            out_shape=(
                jax.ShapeDtypeStruct((16, 8, 4, 256), BF),
                jax.ShapeDtypeStruct((16, 128, 256), BF),
                jax.ShapeDtypeStruct((9, 256, 256), F32),
                jax.ShapeDtypeStruct((3, 256, 256), F32),
                jax.ShapeDtypeStruct((4, 256, 256), F32),
            ),
            in_specs=[vmem] * 3,
            out_specs=(hbm,) * 5,
            scratch_shapes=[
                pltpu.VMEM((16, 256, 256), F32),
                pltpu.VMEM((16, 8, 4, 256), BF),
                pltpu.SemaphoreType.DMA((18,)),
            ],
            compiler_params=pltpu.CompilerParams(vmem_limit_bytes=24 * 1024 * 1024),
        )(down, gx, full)
        return (
            down,
            gx.reshape(16, 16, 8, 256),
            gsp.reshape(3, 3, 256, 256),
            gt,
            gd.reshape(2, 2, 256, 256),
        )

    return jax.shard_map(
        body,
        mesh=mesh,
        in_specs=(P("tm", "grp", None, None), P("tm"), P(), P(), P(), P("tm", "grp", None, None)),
        out_specs=(P("tm", "grp", None, None), P("tm", "grp", None, None), P(), P(), P()),
        check_vma=False,
    )
```
